128 devices in a mesh: grp: 8 (over x, core), mem: 16 (over z, y).
Axes of the slice: x: 4, y: 4, z: 4, core: 2. Of those that a mesh axis runs over, the one named last changes fastest.
Arguments:
- embeddings: bfloat16 [65536, 768], P(('grp', 'mem')), may hold values from -1500 to 1500
- cluster_id: int32 [65536], P(('grp', 'mem')), may hold values from 0 to 7, as said below
- row_order: int32 [65536], P(('grp', 'mem')), may hold values from 0 to 65535, each once
- assignment: int32 [8], replicated, may hold values from 0 to 7, as said below
- placement: int32 [65536], P(('grp', 'mem')), may hold values from 0 to 15
Outputs:
- owner_best: float32 [131072], P(('grp', 'mem'))
The draws below stay inside these ranges and needn't reach their ends.
Inputs may be any that keep to these rules, and one draw needn't show every extreme that they name: `cluster_id`: owner = assignment * 16 + placement; at most 8 rows of one device share an owner, and in every draw some owner gets exactly 8 rows from every device. `assignment`: each group owns exactly 1 cluster.
All inputs are finite; a program needn't handle non-finite values.
Results may differ from the reference program's by a relative error of at most 0.00034.
Values may be sent and summed in bfloat16 or wider, within the bound.
No kernel may reach another device: no remote copies, remote signals or barrier semaphores. Data moves between devices by JAX's collectives and lax.ppermute only.
A program may use at most 128 MiB of HBM per device.

```python
import math
import jax
import jax.numpy as jnp
from jax import lax

D = 768
ROWS_DEV = 512
CL_GRP = 1
GROUPS = 8
MEMBERS = 16
OWNERS = 128
CAP = 8
SLOTS = 1024
ROWS = 65536
CLUSTERS = 8


def route_plan(key):
    base_key = jax.random.fold_in(key, 5)
    key_perm, key_hot, key_dest, key_pick = jax.random.split(base_key, 4)
    shuffled = jax.random.permutation(key_perm, CLUSTERS)
    assignment = shuffled % GROUPS
    listing = jnp.argsort(shuffled)
    hot_owner = jax.random.randint(key_hot, (), 0, OWNERS)
    others = jnp.arange((OWNERS - 1) * CAP) // CAP
    others = others + (others >= hot_owner).astype(others.dtype)

    def per_source(source_key):
        key_take, key_mix = jax.random.split(source_key)
        picked = jax.random.permutation(key_take, (OWNERS - 1) * CAP)[:ROWS_DEV - CAP]
        targets = jnp.concatenate([jnp.full((CAP,), hot_owner, others.dtype), others[picked]])
        return jax.random.permutation(key_mix, targets)
    targets = jax.vmap(per_source)(jax.random.split(key_dest, OWNERS)).reshape(ROWS)
    within = jax.random.randint(key_pick, (ROWS,), 0, CL_GRP)
    cluster_id = listing[targets // MEMBERS + GROUPS * within]
    placement = targets % MEMBERS
    return (cluster_id.astype(jnp.int32), assignment.astype(jnp.int32), placement.astype(jnp.int32))


def draw_cluster_id(key, part):
    return route_plan(key)[0]


def draw_assignment(key, part):
    return route_plan(key)[1]


def draw_placement(key, part):
    return route_plan(key)[2]


def draw_embeddings(key, part):
    cluster_id = route_plan(key)[0]
    key_base, key_shared, key_weight, key_scale = jax.random.split(jax.random.fold_in(key, 11), 4)
    noise = jax.random.truncated_normal(key_base, -4.0, 4.0, (ROWS, D), jnp.float32)
    shared = jax.random.truncated_normal(key_shared, -4.0, 4.0, (ROWS, D), jnp.float32)
    sorter = jnp.argsort(cluster_id, stable=True)
    sorted_ids = cluster_id[sorter]
    position = jnp.arange(ROWS)
    partner = jnp.minimum(position ^ 1, ROWS - 1)
    paired = sorted_ids[partner] == sorted_ids
    anchor_sorted = jnp.where(paired, sorter[jnp.minimum(position, partner)], sorter)
    anchor = jnp.zeros((ROWS,), jnp.int32).at[sorter].set(anchor_sorted.astype(jnp.int32))
    weight = jax.random.uniform(key_weight, (ROWS, 1), jnp.float32, 1.0, 4.0)
    values = noise + weight * shared[anchor]
    row_scale = jnp.exp(jax.random.uniform(key_scale, (ROWS, 1), jnp.float32, 0.0, 2.302585))
    return (values * row_scale).astype(jnp.bfloat16)


def setup_inputs(seed: int = 0) -> dict:
    seeds = jax.random.split(jax.random.key(seed), 6)
    embeddings = draw_embeddings(jax.random.fold_in(seeds[5], 71), 0)
    cluster_id = draw_cluster_id(jax.random.fold_in(seeds[5], 71), 0)
    row_order = jax.random.permutation(seeds[2], ROWS).astype(jnp.int32)
    assignment = draw_assignment(jax.random.fold_in(seeds[5], 71), 0)
    placement = draw_placement(jax.random.fold_in(seeds[5], 71), 0)
    return dict(embeddings=embeddings, cluster_id=cluster_id, row_order=row_order, assignment=assignment, placement=placement)


def reference(embeddings, cluster_id, row_order, assignment, placement):
    widened = embeddings.astype(jnp.float32)
    feature_count = widened.shape[1]
    rounded = (widened * lax.rsqrt(lax.optimization_barrier(jnp.mean(widened * widened, axis=1, keepdims=True)) + 1e-06) * (1.0 / math.sqrt(feature_count))).astype(jnp.bfloat16)
    unit_rows = lax.optimization_barrier(rounded).astype(jnp.float32)
    row_count = unit_rows.shape[0]
    block_rows = 512 if row_count % 512 == 0 else row_count
    blocks = row_count // block_rows

    def block_max(packed):
        block_units, block_cluster, block_order = packed
        scores = jnp.dot(block_units, unit_rows.T, precision=lax.Precision.HIGHEST)
        eligible = (block_cluster[:, None] == cluster_id[None, :]) & (row_order[None, :] < block_order[:, None])
        return jnp.maximum(lax.optimization_barrier(jnp.max(jnp.where(eligible, scores, -2.0), axis=1)), -1.0)
    similar = lax.map(block_max, (unit_rows.reshape(blocks, block_rows, feature_count), cluster_id.reshape(blocks, block_rows), row_order.reshape(blocks, block_rows))).reshape(row_count)
    owner_id = (assignment[cluster_id] * MEMBERS + placement).astype(jnp.int32).reshape(OWNERS, ROWS_DEV)
    owner_hits = (owner_id[:, :, None] == jnp.arange(OWNERS).astype(jnp.int32)[None, None, :]).astype(jnp.int32)
    rank_in_source = lax.optimization_barrier(jnp.sum((jnp.cumsum(owner_hits, axis=1) - 1) * owner_hits, axis=2)).astype(jnp.int32)
    source_id = jnp.arange(OWNERS).astype(jnp.int32)[:, None]
    slot_index = (owner_id * SLOTS + source_id * CAP + rank_in_source).reshape(row_count).astype(jnp.int32)
    return jnp.full((OWNERS * SLOTS,), -1.0, jnp.float32).at[slot_index].set(similar)
```

```python
import math

import jax
import jax.numpy as jnp
from jax import lax
from jax.experimental import pallas as pl
from jax.experimental.pallas import tpu as pltpu
from jax.sharding import Mesh
from jax.sharding import PartitionSpec as P

F32, BF16, I32 = jnp.float32, jnp.bfloat16, jnp.int32
AXES = ("x", "core", "z", "y")
WIDTH = 768
ROWS = 512
KINDS = 8
MEMBERS = 16
CAP = 8
SEND = 96
BLOCK = SEND + 8
PACKED = 640
HELD = PACKED - 16
FAR = 256.0
VMEM = 56 * 2**20


def iota(shape, axis):
    return lax.broadcasted_iota(I32, shape, axis)


def iota_f(shape, axis):
    return iota(shape, axis).astype(F32)


def hot(hits):
    return jnp.where(hits, 1.0, 0.0).astype(BF16)


def mul(a, b):
    return jnp.dot(a, b, preferred_element_type=F32)


def mul_nt(a, b):
    return lax.dot_general(a, b, (((1,), (1,)), ((), ())), preferred_element_type=F32)


def rows_of(*rows):
    n = next(r.shape[1] for r in rows if r is not None)
    at = iota((8, n), 0)
    out = jnp.zeros((8, n), F32)
    for i, row in enumerate(rows):
        if row is not None:
            out = jnp.where(at == i, jnp.broadcast_to(row, (8, n)), out)
    return out


def prep_kernel(assign_ref, emb_ref, cid_ref, order_ref, place_ref, out_ref):
    wide = emb_ref[...].astype(F32)
    mean = jnp.mean(wide * wide, axis=1, keepdims=True)
    unit = (wide * lax.rsqrt(mean + 1e-06) * (1.0 / math.sqrt(WIDTH))).astype(BF16)
    cid = cid_ref[...]
    group = jnp.zeros_like(cid)
    for c in range(KINDS):
        group = jnp.where(cid == c, assign_ref[c], group)
    group = group.astype(F32)
    place = place_ref[...].astype(F32)
    owner = group * MEMBERS + place
    columns = jnp.transpose(rows_of(group, owner))
    before = iota((ROWS, ROWS), 0) < iota((ROWS, ROWS), 1)

    def rank(column, row):
        return jnp.sum(jnp.where(before & (column == row), 1.0, 0.0), axis=0, keepdims=True)

    in_group = rank(columns[:, 0:1], group)
    in_owner = rank(columns[:, 1:2], owner)
    fits = in_group < SEND
    order = order_ref[...]
    high = (order // 256).astype(F32)
    low = (order % 256).astype(F32)
    numbers = rows_of(high, low, place * CAP + in_owner + 1.0).astype(BF16)
    slot = jnp.where(fits, group * 128 + in_group, -1.0)
    spread = mul_nt(numbers, hot(iota_f((KINDS * 128, ROWS), 0) == slot))
    lane = iota((8, 128), 1)
    line = iota((8, 128), 0)
    counts = jnp.zeros((8, 128), F32)
    for g in range(KINDS):
        count = jnp.sum(jnp.where(group == g, 1.0, 0.0), axis=1, keepdims=True)
        counts = jnp.where((lane == g) & (line == 3), count, counts)
    numbers = jnp.concatenate(
        [spread[:, g * 128 : (g + 1) * 128] + counts for g in range(KINDS)]
        + [jnp.zeros((64, 128), F32)],
        axis=0,
    )
    numbers = jnp.concatenate([numbers, jnp.zeros((128, WIDTH - 128), F32)], axis=1).astype(BF16)
    at = iota((1, 128), 1)
    at = jnp.where(at < 64, (at // 8) * BLOCK + SEND + at % 8, -1).astype(F32)
    target = jnp.concatenate([jnp.where(fits, group * BLOCK + in_group, -1.0), at], axis=1)
    placing = hot(iota_f((KINDS * BLOCK, ROWS + 128), 0) == target)
    out_ref[...] = mul(placing, jnp.concatenate([unit, numbers], axis=0)).astype(BF16)


def pack_kernel(in_ref, out_ref):
    count = KINDS * BLOCK
    at = iota((64, count), 0)
    pick = hot(iota((64, count), 1) == (at // 8) * BLOCK + SEND + at % 8)
    numbers = mul(pick, in_ref[:, 0:128])
    lane = iota_f((1, count), 1)
    position = jnp.full((1, count), -1.0, F32)
    slot = iota_f((128, PACKED), 0)
    shift = iota_f((128, PACKED), 1) - slot
    base = jnp.zeros((1, 1), F32)
    gathered = jnp.zeros((8, PACKED), F32)
    line = iota((8, 128), 0)
    over = jnp.zeros((1, 128), F32)
    total = jnp.zeros((1, 128), F32)
    for s in range(KINDS):
        mine = numbers[s * 8 : s * 8 + 8, :]
        n = jnp.sum(jnp.where(mine[2:3, :] > 0.0, 1.0, 0.0), axis=1, keepdims=True)
        step = lane - s * BLOCK
        position = jnp.where((step >= 0.0) & (step < n), base + step, position)
        move = hot((shift == base) & (slot < n))
        mine = jnp.where(line == 4, float(s), mine)
        gathered = gathered + mul(mine.astype(BF16), move)
        base = base + n
        counts = mine[3:4, :]
        over = jnp.maximum(over, jnp.where(counts > SEND, 1.0, 0.0))
        total = total + counts
    over = jnp.maximum(over, jnp.where(total > HELD, 1.0, 0.0))
    over = jnp.max(over, axis=1, keepdims=True)
    position = jnp.where(position < HELD, position, -1.0)
    placing = hot(iota_f((HELD, count), 0) == position)
    out_ref[0:HELD, :] = mul(placing, in_ref[...]).astype(BF16)
    code = gathered[2:3, :]
    valid = (code > 0.0) & (iota((1, PACKED), 1) < HELD)
    final = rows_of(
        jnp.where(valid, gathered[0:1, :], FAR),
        jnp.where(valid, gathered[1:2, :], 0.0),
        jnp.where(valid, code, 0.0),
        jnp.where(valid, gathered[4:5, :], 0.0),
        jnp.broadcast_to(over, (1, PACKED)),
    )
    final = jnp.concatenate([final, jnp.zeros((8, WIDTH - PACKED), F32)], axis=1)
    final = jnp.concatenate([final, jnp.zeros((8, WIDTH), F32)], axis=0)
    out_ref[HELD:PACKED, :] = final.astype(BF16)


TILE = 160


def numbers_of(ref):
    return ref[HELD:PACKED, :].astype(F32)[0:8, 0:PACKED]


def orders_of(numbers):
    return numbers[0:1, :] * 256.0 + numbers[1:2, :]


def pair_max(row_refs, col_refs, best_ref, first, order_ref, init):
    col_orders = [orders_of(numbers_of(c)) for c in col_refs]
    for i, row_ref in enumerate(row_refs):
        order_ref[...] = jnp.transpose(rows_of(orders_of(numbers_of(row_ref))))

        def tile(t, _, row_ref=row_ref, start=(first + i) * PACKED):
            here = pl.ds(pl.multiple_of(t * TILE, TILE), TILE)
            there = pl.ds(pl.multiple_of(start + t * TILE, TILE), TILE)
            rows = row_ref[here, :]
            order = order_ref[here, 0:1]
            best = jnp.full((TILE, 128), -2.0, F32) if init else best_ref[there, :]
            for col_ref, col_order in zip(col_refs, col_orders):
                scores = mul_nt(rows, col_ref[...])
                scores = jnp.where(col_order < order, scores, -2.0)
                for j in range(PACKED // 128):
                    best = jnp.maximum(best, scores[:, j * 128 : (j + 1) * 128])
            best_ref[there, :] = best
            return 0

        lax.fori_loop(0, PACKED // TILE, tile, 0)


def near_kernel(own, y1, y3, z1, z3, best_ref, order_ref):
    pair_max((own, y1, y3), (own, z1, z3), best_ref, 0, order_ref, True)


def far_kernel(own, y1, y3, y2a, y2b, z1, z3, z2a, z2b, near_ref, out_ref, y2, z2, best_ref, order_ref, sent):
    half = PACKED // 2
    y2[0:half, :] = y2a[...]
    y2[half:PACKED, :] = y2b[...]
    z2[0:half, :] = z2a[...]
    z2[half:PACKED, :] = z2b[...]
    best_ref[0 : 3 * PACKED, :] = near_ref[...]
    pair_max((own, y1, y3), (z2,), best_ref, 0, order_ref, False)
    pair_max((y2,), (own, z1, z3, z2), best_ref, 3, order_ref, True)
    over = jnp.zeros((1, 128), F32)
    for ref in (own, y1, y3, y2, z1, z3, z2):
        over = jnp.maximum(over, numbers_of(ref)[4:5, 0:128])
    sent[...] = jnp.zeros((128, 128), F32)
    sent[4 * KINDS : 4 * KINDS + 8, :] = jnp.broadcast_to(over, (8, 128))
    lane = iota_f((1, 128), 1)
    for q, ref in enumerate((own, y1, y3, y2)):
        best = jnp.max(best_ref[q * PACKED : (q + 1) * PACKED, :], axis=1, keepdims=True)
        best = jnp.maximum(best, -1.0)
        numbers = numbers_of(ref)
        code = jnp.transpose(rows_of(numbers[3:4, :] * 128.0 + numbers[2:3, :] - 1.0, numbers[2:3, :]))
        code = jnp.where(code[:, 1:2] > 0.0, code[:, 0:1], -1.0)
        lines = [
            jnp.max(jnp.where(code == lane + 128.0 * s, best, -1.0), axis=0, keepdims=True)
            for s in range(KINDS)
        ]
        sent[q * KINDS : (q + 1) * KINDS, :] = rows_of(*lines)
    out_ref[...] = jnp.transpose(sent[...])


def final_kernel(in_ref, out_ref, over_ref):
    got = jnp.transpose(in_ref[...])
    over_ref[0, 0] = (jnp.max(got[4 * KINDS : 4 * KINDS + 1, :]) > 0.5).astype(I32)
    lane = iota((KINDS, 128), 1) % 32
    best = got[0:KINDS, :]
    for q, away in ((1, 3), (2, 1), (3, 2)):
        part = got[q * KINDS : (q + 1) * KINDS, :]
        moved = jnp.where(
            lane >= 8 * away,
            pltpu.roll(part, 8 * away, 1),
            pltpu.roll(part, 128 + 8 * away - 32, 1),
        )
        best = jnp.maximum(best, moved)
    out_ref[...] = best


def call(kernel, out, scratch=(), ins=None, outs=None, cost=None):
    more = {}
    if ins is not None:
        more["in_specs"] = ins
    if outs is not None:
        more["out_specs"] = outs
    return pl.pallas_call(
        kernel,
        out_shape=out,
        scratch_shapes=list(scratch),
        cost_estimate=cost,
        compiler_params=pltpu.CompilerParams(vmem_limit_bytes=VMEM),
        **more,
    )


def ring(x, axis, step):
    return lax.ppermute(x, axis, [(i, (i + step) % 4) for i in range(4)])


def fast(embeddings, cluster_id, row_order, assignment, placement):
    vmem = pl.BlockSpec(memory_space=pltpu.VMEM)
    smem = pl.BlockSpec(memory_space=pltpu.SMEM)
    line = lambda a: a.reshape(1, ROWS)
    sent = call(
        prep_kernel,
        jax.ShapeDtypeStruct((KINDS * BLOCK, WIDTH), BF16),
        ins=[smem] + [vmem] * 4,
        cost=pl.CostEstimate(flops=10**9, bytes_accessed=2 * 10**6, transcendentals=0),
    )(assignment, embeddings, line(cluster_id), line(row_order), line(placement))
    got = lax.all_to_all(
        sent.reshape(KINDS, BLOCK, WIDTH), ("x", "core"), split_axis=0, concat_axis=0, tiled=True
    )
    own = call(
        pack_kernel,
        jax.ShapeDtypeStruct((PACKED, WIDTH), BF16),
        cost=pl.CostEstimate(flops=10**9, bytes_accessed=2 * 10**6, transcendentals=0),
    )(got.reshape(KINDS * BLOCK, WIDTH))
    half = PACKED // 2
    y1, y3, z1, z3 = ring(own, "y", 1), ring(own, "y", -1), ring(own, "z", 1), ring(own, "z", -1)
    y2a, y2b = ring(y1[:half], "y", 1), ring(y3[half:], "y", -1)
    z2a, z2b = ring(z1[:half], "z", 1), ring(z3[half:], "z", -1)
    pair = 2 * PACKED * PACKED * WIDTH
    near = call(
        near_kernel,
        jax.ShapeDtypeStruct((3 * PACKED, 128), F32),
        [pltpu.VMEM((PACKED, 8), F32)],
        cost=pl.CostEstimate(flops=9 * pair, bytes_accessed=6 * 10**6, transcendentals=0),
    )(own, y1, y3, z1, z3)
    part = pltpu.VMEM((PACKED, WIDTH), BF16)
    back = call(
        far_kernel,
        jax.ShapeDtypeStruct((128, 128), F32),
        [part, part, pltpu.VMEM((4 * PACKED, 128), F32), pltpu.VMEM((PACKED, 8), F32), pltpu.VMEM((128, 128), F32)],
        cost=pl.CostEstimate(flops=7 * pair, bytes_accessed=8 * 10**6, transcendentals=0),
    )(own, y1, y3, y2a, y2b, z1, z3, z2a, z2b, near)
    back = lax.all_to_all(back, ("z", "y"), split_axis=0, concat_axis=0, tiled=True)
    best, over = call(
        final_kernel,
        (jax.ShapeDtypeStruct((KINDS, 128), F32), jax.ShapeDtypeStruct((1, 1), I32)),
        ins=[vmem],
        outs=(vmem, smem),
    )(back)
    return best.reshape(KINDS * 128), over[0, 0] > 0


def slow(embeddings, cluster_id, row_order, assignment, placement):
    owners = KINDS * MEMBERS
    slots = owners * CAP
    wide = embeddings.astype(F32)
    mean = jnp.mean(wide * wide, axis=1, keepdims=True)
    unit = (wide * lax.rsqrt(mean + 1e-06) * (1.0 / math.sqrt(WIDTH))).astype(BF16)
    owner = jnp.sum(
        jnp.where(cluster_id[:, None] == jnp.arange(KINDS, dtype=I32)[None, :], assignment[None, :], 0), axis=1
    ) * MEMBERS + placement
    ids = jnp.arange(ROWS, dtype=I32)
    rank = jnp.sum(((owner[:, None] == owner[None, :]) & (ids[None, :] < ids[:, None])).astype(I32), axis=1)
    target = owner * CAP + rank
    units = jnp.zeros((slots, WIDTH), BF16).at[target].set(unit)
    orders = jnp.full((slots,), ROWS * owners, I32).at[target].set(row_order)
    swap = lambda a: lax.all_to_all(a, AXES, split_axis=0, concat_axis=0, tiled=True)
    units, orders = swap(units), swap(orders)

    def step(_, carried):
        best, piece, piece_orders = carried

        def block(packed):
            block_units, block_orders = packed
            scores = jnp.einsum("ik,jk->ij", block_units, piece, preferred_element_type=F32)
            fit = piece_orders[None, :] < block_orders[:, None]
            return jnp.max(jnp.where(fit, scores, -2.0), axis=1)

        here = lax.map(block, (units.reshape(2, slots // 2, WIDTH), orders.reshape(2, slots // 2)))
        best = jnp.maximum(best, here.reshape(slots))
        turn = [(i, (i + 1) % MEMBERS) for i in range(MEMBERS)]
        return best, lax.ppermute(piece, ("z", "y"), turn), lax.ppermute(piece_orders, ("z", "y"), turn)

    best = lax.fori_loop(0, MEMBERS, step, (jnp.full((slots,), -2.0, F32), units, orders))[0]
    return jnp.where(orders < ROWS * owners, jnp.maximum(best, -1.0), -1.0)


def local(*args):
    best, over = fast(*args)
    return lax.cond(over, lambda args, best: slow(*args), lambda args, best: best, args, best)


def solution(mesh):
    fine = Mesh(mesh.devices.reshape(4, 2, 4, 4), AXES)
    return jax.shard_map(
        local,
        mesh=fine,
        in_specs=(P(AXES, None), P(AXES), P(AXES), P(), P(AXES)),
        out_specs=P(AXES),
        check_vma=False,
    )
```

```python
import math

import jax
import jax.numpy as jnp
from jax import lax
from jax.experimental import pallas as pl
from jax.experimental.pallas import tpu as pltpu
from jax.sharding import Mesh
from jax.sharding import PartitionSpec as P

F32, BF16, I32 = jnp.float32, jnp.bfloat16, jnp.int32
AXES = ("x", "core", "z", "y")
WIDTH = 768
ROWS = 512
KINDS = 8
MEMBERS = 16
CAP = 8
SEND = 96
BLOCK = SEND + 8
PACKED = 640
HELD = PACKED - 16
FAR = 256.0
VMEM = 56 * 2**20


def iota(shape, axis):
    return lax.broadcasted_iota(I32, shape, axis)


def iota_f(shape, axis):
    return iota(shape, axis).astype(F32)


def hot(hits):
    return jnp.where(hits, 1.0, 0.0).astype(BF16)


def mul(a, b):
    return jnp.dot(a, b, preferred_element_type=F32)


def mul_nt(a, b):
    return lax.dot_general(a, b, (((1,), (1,)), ((), ())), preferred_element_type=F32)


def rows_of(*rows):
    n = next(r.shape[1] for r in rows if r is not None)
    at = iota((8, n), 0)
    out = jnp.zeros((8, n), F32)
    for i, row in enumerate(rows):
        if row is not None:
            out = jnp.where(at == i, jnp.broadcast_to(row, (8, n)), out)
    return out


def prep_kernel(assign_ref, emb_ref, cid_ref, order_ref, place_ref, same_ref, other_ref):
    wide = emb_ref[...].astype(F32)
    mean = jnp.mean(wide * wide, axis=1, keepdims=True)
    unit = (wide * lax.rsqrt(mean + 1e-06) * (1.0 / math.sqrt(WIDTH))).astype(BF16)
    my_x, my_core = lax.axis_index("x"), lax.axis_index("core")
    cid = cid_ref[...]
    group = jnp.zeros_like(cid)
    for c in range(KINDS):
        away = lax.rem(assign_ref[c] // 2 - my_x + 4, 4)
        away += 4 * lax.rem(assign_ref[c] + my_core, 2)
        group = jnp.where(cid == c, away, group)
    group = group.astype(F32)
    place = place_ref[...].astype(F32)
    owner = group * MEMBERS + place
    columns = jnp.transpose(rows_of(group, owner))
    before = iota((ROWS, ROWS), 0) < iota((ROWS, ROWS), 1)

    def rank(column, row):
        return jnp.sum(jnp.where(before & (column == row), 1.0, 0.0), axis=0, keepdims=True)

    in_group = rank(columns[:, 0:1], group)
    in_owner = rank(columns[:, 1:2], owner)
    fits = in_group < SEND
    order = order_ref[...]
    high = (order // 256).astype(F32)
    low = (order % 256).astype(F32)
    kind = jnp.where(iota_f((KINDS, ROWS), 0) == group, 1.0, 0.0)
    numbers = jnp.concatenate([kind * high, kind * low, kind * (place * CAP + in_owner + 1.0)], axis=0)
    slot = jnp.transpose(rows_of(in_group))[:, 0:1]
    spread = mul(numbers.astype(BF16), hot(iota_f((ROWS, 128), 1) == slot))
    spread = jnp.where(iota((24, 128), 1) < SEND, spread, 0.0)
    counts = jnp.zeros((KINDS, 128), F32)
    for c in range(KINDS):
        count = jnp.sum(jnp.where(cid == c, 1.0, 0.0), axis=1, keepdims=True)
        counts = jnp.where(iota((KINDS, 128), 1) == assign_ref[c], count, counts)
    numbers = jnp.concatenate([spread, counts, jnp.zeros((96, 128), F32)], axis=0)
    numbers = jnp.concatenate([numbers, jnp.zeros((128, WIDTH - 128), F32)], axis=1).astype(BF16)
    at = iota((1, 128), 1)
    at = jnp.where(at < 32, (at % 8) * BLOCK + SEND + at // 8, -1).astype(F32)
    target = jnp.concatenate([jnp.where(fits, group * BLOCK + in_group, -1.0), at], axis=1)
    both = jnp.concatenate([unit, numbers], axis=0)
    half = 4 * BLOCK
    for ref, first in ((other_ref, half), (same_ref, 0)):
        placing = hot(iota_f((half, ROWS + 128), 0) == target - first)
        ref[...] = mul(placing, both).astype(BF16)


def pack_kernel(here_ref, from1_ref, from2_ref, from3_ref, out_ref, in_ref):
    count = KINDS * BLOCK
    for k, ref in enumerate((here_ref, from1_ref, from2_ref, from3_ref)):
        in_ref[k * 2 * BLOCK : (k + 1) * 2 * BLOCK, :] = ref[...]
    my_x, my_core = lax.axis_index("x"), lax.axis_index("core")
    at = iota((32, count), 0)
    pick = hot(iota((32, count), 1) == (at % 8) * BLOCK + SEND + at // 8)
    numbers = mul(pick, in_ref[:, 0:128])
    n = jnp.sum(jnp.where(numbers[16:24, :] > 0.0, 1.0, 0.0), axis=1, keepdims=True)
    line = iota((KINDS, 1), 0)
    base = jnp.zeros((KINDS, 1), F32)
    source = jnp.zeros((KINDS, 1), F32)
    lane = iota_f((1, count), 1)
    position = jnp.full((1, count), -1.0, F32)
    start = jnp.zeros((1, 1), F32)
    for b in range(KINDS):
        step = lane - b * BLOCK
        mine = n[b : b + 1, :]
        position = jnp.where((step >= 0.0) & (step < mine), start + step, position)
        base = jnp.where(line == b, start, base)
        from_device = 2 * lax.rem(my_x - b // 2 + 4, 4) + lax.rem(my_core + b % 2, 2)
        source = jnp.where(line == b, from_device.astype(F32), source)
        start = start + mine
    position = jnp.where(position < HELD, position, -1.0)
    placing = hot(iota_f((HELD, count), 0) == position)
    out_ref[0:HELD, :] = mul(placing, in_ref[...]).astype(BF16)
    step = iota_f((KINDS, PACKED), 1) - base
    mine = jnp.where((step >= 0.0) & (step < n), 1.0, 0.0)
    slot = jnp.sum(mine * step, axis=0, keepdims=True)
    found = mul(numbers[0:24, :].astype(BF16), hot(iota_f((128, PACKED), 0) == slot))
    high, low, code = (
        jnp.sum(mine * found[i * 8 : i * 8 + 8, :], axis=0, keepdims=True) for i in range(3)
    )
    source = jnp.sum(mine * source, axis=0, keepdims=True)
    counts = numbers[24:32, :]
    over = jnp.max(jnp.where(counts > SEND, 1.0, 0.0), axis=0, keepdims=True)
    over = jnp.maximum(over, jnp.where(jnp.sum(counts, axis=0, keepdims=True) > HELD, 1.0, 0.0))
    over = jnp.max(over, axis=1, keepdims=True)
    valid = (code > 0.0) & (iota((1, PACKED), 1) < HELD)
    final = rows_of(
        jnp.where(valid, high, FAR),
        jnp.where(valid, low, 0.0),
        jnp.where(valid, code, 0.0),
        jnp.where(valid, source, 0.0),
        jnp.broadcast_to(over, (1, PACKED)),
    )
    final = jnp.concatenate([final, jnp.zeros((8, WIDTH - PACKED), F32)], axis=1)
    final = jnp.concatenate([final, jnp.zeros((8, WIDTH), F32)], axis=0)
    out_ref[HELD:PACKED, :] = final.astype(BF16)


def numbers_of(ref):
    n = ref.shape[0]
    return ref[n - 16 : n, :].astype(F32)[0:8, 0:PACKED]


def orders_of(numbers):
    return numbers[0:1, :] * 256.0 + numbers[1:2, :]


def earlier_max(best, rows_ref, row_order, cols_ref, col_order):
    scores = mul_nt(cols_ref[...], rows_ref[...])
    scores = jnp.where(col_order < row_order, scores, -2.0)
    count, n = scores.shape
    return jnp.maximum(best, jnp.max(scores.reshape(count // 8, 8, n), axis=0))


def near_kernel(own, y1, y3, z1, z3, best_ref, order_ref):
    cols = (own, z1, z3)
    order_ref[...] = jnp.transpose(rows_of(*[orders_of(numbers_of(c)) for c in cols]))
    for i, rows in enumerate((own, y1, y3)):
        order = orders_of(numbers_of(rows))
        best = jnp.full((8, PACKED), -2.0, F32)
        for k, col in enumerate(cols):
            best = earlier_max(best, rows, order, col, order_ref[:, k : k + 1])
        best_ref[:, i * PACKED : (i + 1) * PACKED] = best


def far_kernel(own, y1, y3, y2a, y2b, z1, z3, z2a, z2b, near_ref, out_ref, y2, order_ref, sent):
    half = PACKED // 2
    y2[0:half, :] = y2a[...]
    y2[half:PACKED, :] = y2b[...]
    order_ref[...] = jnp.transpose(rows_of(*[orders_of(numbers_of(c)) for c in (own, z1, z3, z2b)]))
    over = jnp.zeros((1, 128), F32)
    for ref in (own, y1, y3, y2b, z1, z3, z2b):
        over = jnp.maximum(over, numbers_of(ref)[4:5, 0:128])
    sent[...] = jnp.zeros((128, 128), F32)
    sent[4 * KINDS : 4 * KINDS + 8, :] = jnp.broadcast_to(over, (8, 128))
    for q, rows in enumerate((own, y1, y3, y2)):
        numbers = numbers_of(rows)
        order = orders_of(numbers)
        if q < 3:
            best = near_ref[:, q * PACKED : (q + 1) * PACKED]
        else:
            best = jnp.full((8, PACKED), -2.0, F32)
            for k, col in enumerate((own, z1, z3)):
                best = earlier_max(best, rows, order, col, order_ref[:, k : k + 1])
        best = earlier_max(best, rows, order, z2a, order_ref[0:half, 3:4])
        best = earlier_max(best, rows, order, z2b, order_ref[half:PACKED, 3:4])
        best = jnp.maximum(jnp.max(best, axis=0, keepdims=True), -1.0)
        high = best.astype(BF16).astype(F32)
        low = best - high
        middle = low.astype(BF16).astype(F32)
        low = low - middle
        lines = jnp.where(
            (iota_f((KINDS, PACKED), 0) == numbers[3:4, :]) & (numbers[2:3, :] > 0.0), 1.0, 0.0
        )
        pieces = jnp.concatenate([lines, lines * high, lines * middle, lines * low], axis=0)
        code = jnp.transpose(rows_of(numbers[2:3, :]))[:, 0:1]
        put = mul(pieces.astype(BF16), hot(iota_f((PACKED, 128), 1) == code - 1.0))
        sent[q * KINDS : (q + 1) * KINDS, :] = (
            (put[0:8, :] - 1.0) + (put[8:16, :] + put[16:24, :] + put[24:32, :])
        )
    out_ref[...] = jnp.transpose(sent[...])


def final_kernel(in_ref, out_ref, over_ref):
    got = jnp.transpose(in_ref[...])
    over_ref[0, 0] = (jnp.max(got[4 * KINDS : 4 * KINDS + 1, :]) > 0.5).astype(I32)
    lane = iota((KINDS, 128), 1) % 32
    best = got[0:KINDS, :]
    for q, away in ((1, 3), (2, 1), (3, 2)):
        part = got[q * KINDS : (q + 1) * KINDS, :]
        moved = jnp.where(
            lane >= 8 * away,
            pltpu.roll(part, 8 * away, 1),
            pltpu.roll(part, 128 + 8 * away - 32, 1),
        )
        best = jnp.maximum(best, moved)
    out_ref[...] = best


def call(kernel, out, scratch=(), ins=None, outs=None, cost=None):
    more = {}
    if ins is not None:
        more["in_specs"] = ins
    if outs is not None:
        more["out_specs"] = outs
    return pl.pallas_call(
        kernel,
        out_shape=out,
        scratch_shapes=list(scratch),
        cost_estimate=cost,
        compiler_params=pltpu.CompilerParams(vmem_limit_bytes=VMEM),
        **more,
    )


def ring(x, axis, step):
    return lax.ppermute(x, axis, [(i, (i + step) % 4) for i in range(4)])


def fast(embeddings, cluster_id, row_order, assignment, placement):
    vmem = pl.BlockSpec(memory_space=pltpu.VMEM)
    smem = pl.BlockSpec(memory_space=pltpu.SMEM)
    line = lambda a: a.reshape(1, ROWS)
    cheap = pl.CostEstimate(flops=10**9, bytes_accessed=2 * 10**6, transcendentals=0)
    blocks = jax.ShapeDtypeStruct((4 * BLOCK, WIDTH), BF16)
    same, other = call(
        prep_kernel,
        (blocks, blocks),
        ins=[smem] + [vmem] * 4,
        cost=cheap,
    )(assignment, embeddings, line(cluster_id), line(row_order), line(placement))
    other = lax.ppermute(other, "core", [(0, 1), (1, 0)])
    shape = (4, 1, BLOCK, WIDTH)
    both = jnp.concatenate([same.reshape(shape), other.reshape(shape)], axis=1).reshape(4, 2 * BLOCK, WIDTH)
    own = call(
        pack_kernel,
        jax.ShapeDtypeStruct((PACKED, WIDTH), BF16),
        [pltpu.VMEM((KINDS * BLOCK, WIDTH), BF16)],
        cost=cheap,
    )(both[0], *[ring(both[k], "x", k) for k in (1, 2, 3)])
    half = PACKED // 2
    y1, y3, z1, z3 = ring(own, "y", 1), ring(own, "y", -1), ring(own, "z", 1), ring(own, "z", -1)
    y2a, y2b = ring(y1[:half], "y", 1), ring(y3[half:], "y", -1)
    z2a, z2b = ring(z1[:half], "z", 1), ring(z3[half:], "z", -1)
    pair = 2 * PACKED * PACKED * WIDTH
    near = call(
        near_kernel,
        jax.ShapeDtypeStruct((8, 3 * PACKED), F32),
        [pltpu.VMEM((PACKED, 8), F32)],
        cost=pl.CostEstimate(flops=9 * pair, bytes_accessed=6 * 10**6, transcendentals=0),
    )(own, y1, y3, z1, z3)
    back = call(
        far_kernel,
        jax.ShapeDtypeStruct((128, 128), F32),
        [pltpu.VMEM((PACKED, WIDTH), BF16), pltpu.VMEM((PACKED, 8), F32), pltpu.VMEM((128, 128), F32)],
        cost=pl.CostEstimate(flops=7 * pair, bytes_accessed=8 * 10**6, transcendentals=0),
    )(own, y1, y3, y2a, y2b, z1, z3, z2a, z2b, near)
    back = lax.all_to_all(back, ("z", "y"), split_axis=0, concat_axis=0, tiled=True)
    best, over = call(
        final_kernel,
        (jax.ShapeDtypeStruct((KINDS, 128), F32), jax.ShapeDtypeStruct((1, 1), I32)),
        ins=[vmem],
        outs=(vmem, smem),
    )(back)
    return best.reshape(KINDS * 128), over[0, 0] > 0


def slow(embeddings, cluster_id, row_order, assignment, placement):
    owners = KINDS * MEMBERS
    slots = owners * CAP
    wide = embeddings.astype(F32)
    mean = jnp.mean(wide * wide, axis=1, keepdims=True)
    unit = (wide * lax.rsqrt(mean + 1e-06) * (1.0 / math.sqrt(WIDTH))).astype(BF16)
    owner = jnp.sum(
        jnp.where(cluster_id[:, None] == jnp.arange(KINDS, dtype=I32)[None, :], assignment[None, :], 0), axis=1
    ) * MEMBERS + placement
    ids = jnp.arange(ROWS, dtype=I32)
    rank = jnp.sum(((owner[:, None] == owner[None, :]) & (ids[None, :] < ids[:, None])).astype(I32), axis=1)
    target = owner * CAP + rank
    units = jnp.zeros((slots, WIDTH), BF16).at[target].set(unit)
    orders = jnp.full((slots,), ROWS * owners, I32).at[target].set(row_order)
    swap = lambda a: lax.all_to_all(a, AXES, split_axis=0, concat_axis=0, tiled=True)
    units, orders = swap(units), swap(orders)

    def step(_, carried):
        best, piece, piece_orders = carried

        def block(packed):
            block_units, block_orders = packed
            scores = jnp.einsum("ik,jk->ij", block_units, piece, preferred_element_type=F32)
            fit = piece_orders[None, :] < block_orders[:, None]
            return jnp.max(jnp.where(fit, scores, -2.0), axis=1)

        here = lax.map(block, (units.reshape(2, slots // 2, WIDTH), orders.reshape(2, slots // 2)))
        best = jnp.maximum(best, here.reshape(slots))
        turn = [(i, (i + 1) % MEMBERS) for i in range(MEMBERS)]
        return best, lax.ppermute(piece, ("z", "y"), turn), lax.ppermute(piece_orders, ("z", "y"), turn)

    best = lax.fori_loop(0, MEMBERS, step, (jnp.full((slots,), -2.0, F32), units, orders))[0]
    return jnp.where(orders < ROWS * owners, jnp.maximum(best, -1.0), -1.0)


def local(*args):
    best, over = fast(*args)
    return lax.cond(over, lambda args, best: slow(*args), lambda args, best: best, args, best)


def solution(mesh):
    fine = Mesh(mesh.devices.reshape(4, 2, 4, 4), AXES)
    return jax.shard_map(
        local,
        mesh=fine,
        in_specs=(P(AXES, None), P(AXES), P(AXES), P(), P(AXES)),
        out_specs=P(AXES),
        check_vma=False,
    )
```

```python
import math

import jax
import jax.numpy as jnp
from jax import lax
from jax.experimental import pallas as pl
from jax.experimental.pallas import tpu as pltpu
from jax.sharding import Mesh
from jax.sharding import PartitionSpec as P

F32, BF16, I32 = jnp.float32, jnp.bfloat16, jnp.int32
AXES = ("x", "core", "z", "y")
WIDTH = 768
ROWS = 512
KINDS = 8
MEMBERS = 16
CAP = 8
SEND = 96
BLOCK = SEND + 8
PACKED = 640
HELD = PACKED - 16
FAR = 256.0
VMEM = 16 * 2**20


def iota(shape, axis):
    return lax.broadcasted_iota(I32, shape, axis)


def iota_f(shape, axis):
    return iota(shape, axis).astype(F32)


def hot(hits):
    return jnp.where(hits, 1.0, 0.0).astype(BF16)


def mul(a, b):
    return jnp.dot(a, b, preferred_element_type=F32)


def mul_nt(a, b):
    return lax.dot_general(a, b, (((1,), (1,)), ((), ())), preferred_element_type=F32)


def rows_of(*rows):
    n = next(r.shape[1] for r in rows if r is not None)
    at = iota((8, n), 0)
    out = jnp.zeros((8, n), F32)
    for i, row in enumerate(rows):
        if row is not None:
            out = jnp.where(at == i, jnp.broadcast_to(row, (8, n)), out)
    return out


def prep_kernel(assign_ref, emb_ref, cid_ref, order_ref, place_ref, same_ref, other_ref):
    wide = emb_ref[...].astype(F32)
    mean = jnp.mean(wide * wide, axis=1, keepdims=True)
    unit = (wide * lax.rsqrt(mean + 1e-06) * (1.0 / math.sqrt(WIDTH))).astype(BF16)
    my_x, my_core = lax.axis_index("x"), lax.axis_index("core")
    cid = cid_ref[...]
    group = jnp.zeros_like(cid)
    for c in range(KINDS):
        away = lax.rem(assign_ref[c] // 2 - my_x + 4, 4)
        away += 4 * lax.rem(assign_ref[c] + my_core, 2)
        group = jnp.where(cid == c, away, group)
    group = group.astype(F32)
    place = place_ref[...].astype(F32)
    owner = group * MEMBERS + place
    columns = jnp.transpose(rows_of(group, owner))
    before = iota((ROWS, ROWS), 0) < iota((ROWS, ROWS), 1)

    def rank(column, row):
        return jnp.sum(jnp.where(before & (column == row), 1.0, 0.0), axis=0, keepdims=True)

    in_group = rank(columns[:, 0:1], group)
    in_owner = rank(columns[:, 1:2], owner)
    fits = in_group < SEND
    order = order_ref[...]
    high = (order // 256).astype(F32)
    low = (order % 256).astype(F32)
    kind = jnp.where(iota_f((KINDS, ROWS), 0) == group, 1.0, 0.0)
    numbers = jnp.concatenate([kind * high, kind * low, kind * (place * CAP + in_owner + 1.0)], axis=0)
    slot = jnp.transpose(rows_of(in_group))[:, 0:1]
    spread = mul(numbers.astype(BF16), hot(iota_f((ROWS, 128), 1) == slot))
    spread = jnp.where(iota((24, 128), 1) < SEND, spread, 0.0)
    counts = jnp.zeros((KINDS, 128), F32)
    for c in range(KINDS):
        count = jnp.sum(jnp.where(cid == c, 1.0, 0.0), axis=1, keepdims=True)
        counts = jnp.where(iota((KINDS, 128), 1) == assign_ref[c], count, counts)
    numbers = jnp.concatenate([spread, counts, jnp.zeros((96, 128), F32)], axis=0)
    numbers = jnp.concatenate([numbers, jnp.zeros((128, WIDTH - 128), F32)], axis=1).astype(BF16)
    at = iota((1, 128), 1)
    at = jnp.where(at < 32, (at % 8) * BLOCK + SEND + at // 8, -1).astype(F32)
    target = jnp.concatenate([jnp.where(fits, group * BLOCK + in_group, -1.0), at], axis=1)
    both = jnp.concatenate([unit, numbers], axis=0)
    half = 4 * BLOCK
    for ref, first in ((other_ref, half), (same_ref, 0)):
        placing = hot(iota_f((half, ROWS + 128), 0) == target - first)
        ref[...] = mul(placing, both).astype(BF16)


def pack_kernel(here_ref, from1_ref, from2_ref, from3_ref, out_ref, in_ref):
    count = KINDS * BLOCK
    for k, ref in enumerate((here_ref, from1_ref, from2_ref, from3_ref)):
        in_ref[k * 2 * BLOCK : (k + 1) * 2 * BLOCK, :] = ref[...]
    my_x, my_core = lax.axis_index("x"), lax.axis_index("core")
    at = iota((32, count), 0)
    pick = hot(iota((32, count), 1) == (at % 8) * BLOCK + SEND + at // 8)
    numbers = mul(pick, in_ref[:, 0:128])
    n = jnp.sum(jnp.where(numbers[16:24, :] > 0.0, 1.0, 0.0), axis=1, keepdims=True)
    line = iota((KINDS, 1), 0)
    base = jnp.zeros((KINDS, 1), F32)
    source = jnp.zeros((KINDS, 1), F32)
    lane = iota_f((1, count), 1)
    position = jnp.full((1, count), -1.0, F32)
    start = jnp.zeros((1, 1), F32)
    for b in range(KINDS):
        step = lane - b * BLOCK
        mine = n[b : b + 1, :]
        position = jnp.where((step >= 0.0) & (step < mine), start + step, position)
        base = jnp.where(line == b, start, base)
        from_device = 2 * lax.rem(my_x - b // 2 + 4, 4) + lax.rem(my_core + b % 2, 2)
        source = jnp.where(line == b, from_device.astype(F32), source)
        start = start + mine
    position = jnp.where(position < HELD, position, -1.0)
    placing = hot(iota_f((HELD, count), 0) == position)
    out_ref[0:HELD, :] = mul(placing, in_ref[...]).astype(BF16)
    step = iota_f((KINDS, PACKED), 1) - base
    mine = jnp.where((step >= 0.0) & (step < n), 1.0, 0.0)
    slot = jnp.sum(mine * step, axis=0, keepdims=True)
    found = mul(numbers[0:24, :].astype(BF16), hot(iota_f((128, PACKED), 0) == slot))
    high, low, code = (
        jnp.sum(mine * found[i * 8 : i * 8 + 8, :], axis=0, keepdims=True) for i in range(3)
    )
    source = jnp.sum(mine * source, axis=0, keepdims=True)
    counts = numbers[24:32, :]
    over = jnp.max(jnp.where(counts > SEND, 1.0, 0.0), axis=0, keepdims=True)
    over = jnp.maximum(over, jnp.where(jnp.sum(counts, axis=0, keepdims=True) > HELD, 1.0, 0.0))
    over = jnp.max(over, axis=1, keepdims=True)
    valid = (code > 0.0) & (iota((1, PACKED), 1) < HELD)
    final = rows_of(
        jnp.where(valid, high, FAR),
        jnp.where(valid, low, 0.0),
        jnp.where(valid, code, 0.0),
        jnp.where(valid, source, 0.0),
        jnp.broadcast_to(over, (1, PACKED)),
    )
    final = jnp.concatenate([final, jnp.zeros((8, WIDTH - PACKED), F32)], axis=1)
    final = jnp.concatenate([final, jnp.zeros((8, WIDTH), F32)], axis=0)
    out_ref[HELD:PACKED, :] = final.astype(BF16)


def numbers_of(ref):
    n = ref.shape[0]
    return ref[n - 16 : n, :].astype(F32)[0:8, 0:PACKED]


def orders_of(numbers):
    return numbers[0:1, :] * 256.0 + numbers[1:2, :]


def earlier_max(best, rows_ref, row_order, cols_ref, col_order):
    scores = mul_nt(cols_ref[...], rows_ref[...])
    scores = jnp.where(col_order < row_order, scores, -2.0)
    count, n = scores.shape
    return jnp.maximum(best, jnp.max(scores.reshape(count // 8, 8, n), axis=0))


def near_kernel(own, y1, y3, z1, z3, best_ref, order_ref):
    cols = (own, z1, z3)
    order_ref[...] = jnp.transpose(rows_of(*[orders_of(numbers_of(c)) for c in cols]))
    for i, rows in enumerate((own, y1, y3)):
        order = orders_of(numbers_of(rows))
        best = jnp.full((8, PACKED), -2.0, F32)
        for k, col in enumerate(cols):
            best = earlier_max(best, rows, order, col, order_ref[:, k : k + 1])
        best_ref[:, i * PACKED : (i + 1) * PACKED] = best


def far_kernel(own, y1, y3, y2a, y2b, z1, z3, z2a, z2b, near_ref, out_ref, y2, order_ref, sent):
    half = PACKED // 2
    y2[0:half, :] = y2a[...]
    y2[half:PACKED, :] = y2b[...]
    order_ref[...] = jnp.transpose(rows_of(*[orders_of(numbers_of(c)) for c in (own, z1, z3, z2b)]))
    over = jnp.zeros((1, 128), F32)
    for ref in (own, y1, y3, y2b, z1, z3, z2b):
        over = jnp.maximum(over, numbers_of(ref)[4:5, 0:128])
    sent[...] = jnp.zeros((128, 128), F32)
    sent[4 * KINDS : 4 * KINDS + 8, :] = jnp.broadcast_to(over, (8, 128))
    for q, rows in enumerate((own, y1, y3, y2)):
        numbers = numbers_of(rows)
        order = orders_of(numbers)
        if q < 3:
            best = near_ref[:, q * PACKED : (q + 1) * PACKED]
        else:
            best = jnp.full((8, PACKED), -2.0, F32)
            for k, col in enumerate((own, z1, z3)):
                best = earlier_max(best, rows, order, col, order_ref[:, k : k + 1])
        best = earlier_max(best, rows, order, z2a, order_ref[0:half, 3:4])
        best = earlier_max(best, rows, order, z2b, order_ref[half:PACKED, 3:4])
        best = jnp.maximum(jnp.max(best, axis=0, keepdims=True), -1.0)
        high = best.astype(BF16).astype(F32)
        low = best - high
        middle = low.astype(BF16).astype(F32)
        low = low - middle
        lines = jnp.where(
            (iota_f((KINDS, PACKED), 0) == numbers[3:4, :]) & (numbers[2:3, :] > 0.0), 1.0, 0.0
        )
        pieces = jnp.concatenate([lines, lines * high, lines * middle, lines * low], axis=0)
        code = jnp.transpose(rows_of(numbers[2:3, :]))[:, 0:1]
        put = mul(pieces.astype(BF16), hot(iota_f((PACKED, 128), 1) == code - 1.0))
        sent[q * KINDS : (q + 1) * KINDS, :] = (
            (put[0:8, :] - 1.0) + (put[8:16, :] + put[16:24, :] + put[24:32, :])
        )
    out_ref[...] = jnp.transpose(sent[...])


def final_kernel(in_ref, out_ref, over_ref):
    got = jnp.transpose(in_ref[...])
    over_ref[0, 0] = (jnp.max(got[4 * KINDS : 4 * KINDS + 1, :]) > 0.5).astype(I32)
    lane = iota((KINDS, 128), 1) % 32
    best = got[0:KINDS, :]
    for q, away in ((1, 3), (2, 1), (3, 2)):
        part = got[q * KINDS : (q + 1) * KINDS, :]
        moved = jnp.where(
            lane >= 8 * away,
            pltpu.roll(part, 8 * away, 1),
            pltpu.roll(part, 128 + 8 * away - 32, 1),
        )
        best = jnp.maximum(best, moved)
    out_ref[...] = best


def call(kernel, out, scratch=(), ins=None, outs=None, cost=None):
    more = {}
    if ins is not None:
        more["in_specs"] = ins
    if outs is not None:
        more["out_specs"] = outs
    return pl.pallas_call(
        kernel,
        out_shape=out,
        scratch_shapes=list(scratch),
        cost_estimate=cost,
        compiler_params=pltpu.CompilerParams(vmem_limit_bytes=VMEM),
        **more,
    )


def ring(x, axis, step):
    return lax.ppermute(x, axis, [(i, (i + step) % 4) for i in range(4)])


def fast(embeddings, cluster_id, row_order, assignment, placement):
    vmem = pl.BlockSpec(memory_space=pltpu.VMEM)
    smem = pl.BlockSpec(memory_space=pltpu.SMEM)
    line = lambda a: a.reshape(1, ROWS)
    cheap = pl.CostEstimate(flops=10**9, bytes_accessed=2 * 10**6, transcendentals=0)
    blocks = jax.ShapeDtypeStruct((4 * BLOCK, WIDTH), BF16)
    same, other = call(
        prep_kernel,
        (blocks, blocks),
        ins=[smem] + [vmem] * 4,
        cost=cheap,
    )(assignment, embeddings, line(cluster_id), line(row_order), line(placement))
    other = lax.ppermute(other, "core", [(0, 1), (1, 0)])
    shape = (4, 1, BLOCK, WIDTH)
    both = jnp.concatenate([same.reshape(shape), other.reshape(shape)], axis=1).reshape(4, 2 * BLOCK, WIDTH)
    own = call(
        pack_kernel,
        jax.ShapeDtypeStruct((PACKED, WIDTH), BF16),
        [pltpu.VMEM((KINDS * BLOCK, WIDTH), BF16)],
        cost=cheap,
    )(both[0], *[ring(both[k], "x", k) for k in (1, 2, 3)])
    half = PACKED // 2
    y1, y3, z1, z3 = ring(own, "y", 1), ring(own, "y", -1), ring(own, "z", 1), ring(own, "z", -1)
    y2a, y2b = ring(y1[:half], "y", 1), ring(y3[half:], "y", -1)
    z2a, z2b = ring(z1[:half], "z", 1), ring(z3[half:], "z", -1)
    pair = 2 * PACKED * PACKED * WIDTH
    near = call(
        near_kernel,
        jax.ShapeDtypeStruct((8, 3 * PACKED), F32),
        [pltpu.VMEM((PACKED, 8), F32)],
        cost=pl.CostEstimate(flops=9 * pair, bytes_accessed=6 * 10**6, transcendentals=0),
    )(own, y1, y3, z1, z3)
    back = call(
        far_kernel,
        jax.ShapeDtypeStruct((128, 128), F32),
        [pltpu.VMEM((PACKED, WIDTH), BF16), pltpu.VMEM((PACKED, 8), F32), pltpu.VMEM((128, 128), F32)],
        cost=pl.CostEstimate(flops=7 * pair, bytes_accessed=8 * 10**6, transcendentals=0),
    )(own, y1, y3, y2a, y2b, z1, z3, z2a, z2b, near)
    back = lax.all_to_all(back, ("z", "y"), split_axis=0, concat_axis=0, tiled=True)
    best, over = call(
        final_kernel,
        (jax.ShapeDtypeStruct((KINDS, 128), F32), jax.ShapeDtypeStruct((1, 1), I32)),
        ins=[vmem],
        outs=(vmem, smem),
    )(back)
    return best.reshape(KINDS * 128), over[0, 0] > 0


def slow(embeddings, cluster_id, row_order, assignment, placement):
    owners = KINDS * MEMBERS
    slots = owners * CAP
    wide = embeddings.astype(F32)
    mean = jnp.mean(wide * wide, axis=1, keepdims=True)
    unit = (wide * lax.rsqrt(mean + 1e-06) * (1.0 / math.sqrt(WIDTH))).astype(BF16)
    owner = jnp.sum(
        jnp.where(cluster_id[:, None] == jnp.arange(KINDS, dtype=I32)[None, :], assignment[None, :], 0), axis=1
    ) * MEMBERS + placement
    ids = jnp.arange(ROWS, dtype=I32)
    rank = jnp.sum(((owner[:, None] == owner[None, :]) & (ids[None, :] < ids[:, None])).astype(I32), axis=1)
    target = owner * CAP + rank
    units = jnp.zeros((slots, WIDTH), BF16).at[target].set(unit)
    orders = jnp.full((slots,), ROWS * owners, I32).at[target].set(row_order)
    swap = lambda a: lax.all_to_all(a, AXES, split_axis=0, concat_axis=0, tiled=True)
    units, orders = swap(units), swap(orders)

    def step(_, carried):
        best, piece, piece_orders = carried

        def block(packed):
            block_units, block_orders = packed
            scores = jnp.einsum("ik,jk->ij", block_units, piece, preferred_element_type=F32)
            fit = piece_orders[None, :] < block_orders[:, None]
            return jnp.max(jnp.where(fit, scores, -2.0), axis=1)

        here = lax.map(block, (units.reshape(2, slots // 2, WIDTH), orders.reshape(2, slots // 2)))
        best = jnp.maximum(best, here.reshape(slots))
        turn = [(i, (i + 1) % MEMBERS) for i in range(MEMBERS)]
        return best, lax.ppermute(piece, ("z", "y"), turn), lax.ppermute(piece_orders, ("z", "y"), turn)

    best = lax.fori_loop(0, MEMBERS, step, (jnp.full((slots,), -2.0, F32), units, orders))[0]
    return jnp.where(orders < ROWS * owners, jnp.maximum(best, -1.0), -1.0)


def local(*args):
    best, over = fast(*args)
    return lax.cond(over, lambda args, best: slow(*args), lambda args, best: best, args, best)


def solution(mesh):
    fine = Mesh(mesh.devices.reshape(4, 2, 4, 4), AXES)
    return jax.shard_map(
        local,
        mesh=fine,
        in_specs=(P(AXES, None), P(AXES), P(AXES), P(), P(AXES)),
        out_specs=P(AXES),
        check_vma=False,
    )
```

```python
import math

import jax
import jax.numpy as jnp
from jax import lax
from jax.experimental import pallas as pl
from jax.experimental.pallas import tpu as pltpu
from jax.sharding import Mesh
from jax.sharding import PartitionSpec as P

F32, BF16, I32 = jnp.float32, jnp.bfloat16, jnp.int32
AXES = ("x", "core", "z", "y")
WIDTH = 768
ROWS = 512
KINDS = 8
MEMBERS = 16
CAP = 8
SEND = 96
BLOCK = SEND + 8
PACKED = 640
HELD = PACKED - 16
FAR = 256.0
VMEM = 16 * 2**20


def iota(shape, axis):
    return lax.broadcasted_iota(I32, shape, axis)


def iota_f(shape, axis):
    return iota(shape, axis).astype(F32)


def hot(hits):
    return jnp.where(hits, 1.0, 0.0).astype(BF16)


def mul(a, b):
    return jnp.dot(a, b, preferred_element_type=F32)


def mul_nt(a, b):
    return lax.dot_general(a, b, (((1,), (1,)), ((), ())), preferred_element_type=F32)


def rows_of(*rows):
    n = next(r.shape[1] for r in rows if r is not None)
    at = iota((8, n), 0)
    out = jnp.zeros((8, n), F32)
    for i, row in enumerate(rows):
        if row is not None:
            out = jnp.where(at == i, jnp.broadcast_to(row, (8, n)), out)
    return out


def prep_kernel(assign_ref, emb_ref, cid_ref, order_ref, place_ref, same_ref, other_ref):
    wide = emb_ref[...].astype(F32)
    mean = jnp.mean(wide * wide, axis=1, keepdims=True)
    unit = (wide * lax.rsqrt(mean + 1e-06) * (1.0 / math.sqrt(WIDTH))).astype(BF16)
    my_x, my_core, my_y = lax.axis_index("x"), lax.axis_index("core"), lax.axis_index("y")
    cid = cid_ref[...]
    group = jnp.zeros_like(cid)
    for c in range(KINDS):
        core = lax.rem(assign_ref[c], 2)
        away = lax.rem(assign_ref[c] // 2 - jnp.where(core == 0, my_x, my_y) + 4, 4)
        away += 4 * lax.rem(core + my_core, 2)
        group = jnp.where(cid == c, away, group)
    group = group.astype(F32)
    place = place_ref[...].astype(F32)
    owner = group * MEMBERS + place
    columns = jnp.transpose(rows_of(group, owner))
    before = iota((ROWS, ROWS), 0) < iota((ROWS, ROWS), 1)

    def rank(column, row):
        return jnp.sum(jnp.where(before & (column == row), 1.0, 0.0), axis=0, keepdims=True)

    in_group = rank(columns[:, 0:1], group)
    in_owner = rank(columns[:, 1:2], owner)
    fits = in_group < SEND
    order = order_ref[...]
    high = (order // 256).astype(F32)
    low = (order % 256).astype(F32)
    kind = jnp.where(iota_f((KINDS, ROWS), 0) == group, 1.0, 0.0)
    numbers = jnp.concatenate([kind * high, kind * low, kind * (place * CAP + in_owner + 1.0)], axis=0)
    slot = jnp.transpose(rows_of(in_group))[:, 0:1]
    spread = mul(numbers.astype(BF16), hot(iota_f((ROWS, 128), 1) == slot))
    spread = jnp.where(iota((24, 128), 1) < SEND, spread, 0.0)
    counts = jnp.zeros((KINDS, 128), F32)
    for c in range(KINDS):
        count = jnp.sum(jnp.where(cid == c, 1.0, 0.0), axis=1, keepdims=True)
        counts = jnp.where(iota((KINDS, 128), 1) == assign_ref[c], count, counts)
    numbers = jnp.concatenate([spread, counts, jnp.zeros((96, 128), F32)], axis=0)
    numbers = jnp.concatenate([numbers, jnp.zeros((128, WIDTH - 128), F32)], axis=1).astype(BF16)
    at = iota((1, 128), 1)
    at = jnp.where(at < 32, (at % 8) * BLOCK + SEND + at // 8, -1).astype(F32)
    target = jnp.concatenate([jnp.where(fits, group * BLOCK + in_group, -1.0), at], axis=1)
    both = jnp.concatenate([unit, numbers], axis=0)
    half = 4 * BLOCK
    for ref, first in ((other_ref, half), (same_ref, 0)):
        placing = hot(iota_f((half, ROWS + 128), 0) == target - first)
        ref[...] = mul(placing, both).astype(BF16)


def pack_kernel(here_ref, from1_ref, from2_ref, from3_ref, out_ref, over_ref, in_ref):
    count = KINDS * BLOCK
    for k, ref in enumerate((here_ref, from1_ref, from2_ref, from3_ref)):
        in_ref[k * 2 * BLOCK : (k + 1) * 2 * BLOCK, :] = ref[...]
    my_core = lax.axis_index("core")
    my_line = jnp.where(my_core == 0, lax.axis_index("x"), lax.axis_index("y"))
    at = iota((32, count), 0)
    pick = hot(iota((32, count), 1) == (at % 8) * BLOCK + SEND + at // 8)
    numbers = mul(pick, in_ref[:, 0:128])
    n = jnp.sum(jnp.where(numbers[16:24, :] > 0.0, 1.0, 0.0), axis=1, keepdims=True)
    line = iota((KINDS, 1), 0)
    base = jnp.zeros((KINDS, 1), F32)
    source = jnp.zeros((KINDS, 1), F32)
    lane = iota_f((1, count), 1)
    position = jnp.full((1, count), -1.0, F32)
    start = jnp.zeros((1, 1), F32)
    for b in range(KINDS):
        step = lane - b * BLOCK
        mine = n[b : b + 1, :]
        position = jnp.where((step >= 0.0) & (step < mine), start + step, position)
        base = jnp.where(line == b, start, base)
        from_device = 2 * lax.rem(my_line - b // 2 + 4, 4) + lax.rem(my_core + b % 2, 2)
        source = jnp.where(line == b, from_device.astype(F32), source)
        start = start + mine
    position = jnp.where(position < HELD, position, -1.0)
    placing = hot(iota_f((HELD, count), 0) == position)
    out_ref[0:HELD, :] = mul(placing, in_ref[...]).astype(BF16)
    step = iota_f((KINDS, PACKED), 1) - base
    mine = jnp.where((step >= 0.0) & (step < n), 1.0, 0.0)
    slot = jnp.sum(mine * step, axis=0, keepdims=True)
    found = mul(numbers[0:24, :].astype(BF16), hot(iota_f((128, PACKED), 0) == slot))
    high, low, code = (
        jnp.sum(mine * found[i * 8 : i * 8 + 8, :], axis=0, keepdims=True) for i in range(3)
    )
    source = jnp.sum(mine * source, axis=0, keepdims=True)
    counts = numbers[24:32, :]
    over = jnp.max(jnp.where(counts > SEND, 1.0, 0.0), axis=0, keepdims=True)
    ours = iota((1, 128), 1) % 2 == my_core
    full = ours & (jnp.sum(counts, axis=0, keepdims=True) > HELD)
    over = jnp.maximum(over, jnp.where(full, 1.0, 0.0))
    over = jnp.max(over, axis=1, keepdims=True)
    valid = (code > 0.0) & (iota((1, PACKED), 1) < HELD)
    final = rows_of(
        jnp.where(valid, high, FAR),
        jnp.where(valid, low, 0.0),
        jnp.where(valid, code, 0.0),
        jnp.where(valid, source, 0.0),
    )
    over_ref[...] = jnp.broadcast_to(over, (8, 128))
    final = jnp.concatenate([final, jnp.zeros((8, WIDTH - PACKED), F32)], axis=1)
    final = jnp.concatenate([final, jnp.zeros((8, WIDTH), F32)], axis=0)
    out_ref[HELD:PACKED, :] = final.astype(BF16)


def numbers_of(ref):
    n = ref.shape[0]
    return ref[n - 16 : n, :].astype(F32)[0:8, 0:PACKED]


def orders_of(numbers):
    return numbers[0:1, :] * 256.0 + numbers[1:2, :]


def earlier_max(best, rows_ref, row_order, cols_ref, col_order):
    scores = mul_nt(cols_ref[...], rows_ref[...])
    scores = jnp.where(col_order < row_order, scores, -2.0)
    count, n = scores.shape
    return jnp.maximum(best, jnp.max(scores.reshape(count // 8, 8, n), axis=0))


def orders_down(*refs):
    return jnp.transpose(rows_of(*[orders_of(numbers_of(r)) for r in refs]))


def all_earlier(best, rows, cols, orders, first):
    order = orders_of(numbers_of(rows))
    for k, col in enumerate(cols):
        best = earlier_max(best, rows, order, col, orders[:, first + k : first + k + 1])
    return best


def nothing():
    return jnp.full((8, PACKED), -2.0, F32)


def near_kernel(own, m1, m3, z1, best_ref, order_ref):
    order_ref[...] = orders_down(z1, own, m1, m3)
    for i, rows in enumerate((own, m1, m3)):
        best_ref[i] = all_earlier(nothing(), rows, (z1, own), order_ref, 0)
    best_ref[3] = all_earlier(nothing(), z1, (own, m1, m3), order_ref, 1)


def middle_kernel(own, z1, m2a, m2b, near_ref, m2, best_ref, order_ref):
    half = PACKED // 2
    m2[0:half, :] = m2a[...]
    m2[half:PACKED, :] = m2b[...]
    order_ref[...] = orders_down(z1, own, m2)
    best_ref[0] = all_earlier(nothing(), m2, (z1, own), order_ref, 0)
    best_ref[1] = all_earlier(near_ref[3], z1, (m2,), order_ref, 2)


def to_owners(best, numbers):
    best = jnp.maximum(jnp.max(best, axis=0, keepdims=True), -1.0)
    high = best.astype(BF16).astype(F32)
    low = best - high
    middle = low.astype(BF16).astype(F32)
    low = low - middle
    lines = jnp.where((iota_f((KINDS, PACKED), 0) == numbers[3:4, :]) & (numbers[2:3, :] > 0.0), 1.0, 0.0)
    pieces = jnp.concatenate([lines, lines * high, lines * middle, lines * low], axis=0)
    code = jnp.transpose(rows_of(numbers[2:3, :]))[:, 0:1]
    put = mul(pieces.astype(BF16), hot(iota_f((PACKED, 128), 1) == code - 1.0))
    return (put[0:8, :] - 1.0) + (put[8:16, :] + put[16:24, :] + put[24:32, :])


OVER = 5 * KINDS


def far_kernel(own, m1, m3, m2, z1, z2, near_ref, middle_ref, over_ref, other_over_ref, out_ref, order_ref, sent):
    order_ref[...] = orders_down(z2)
    sent[...] = jnp.zeros((128, 128), F32)
    over = jnp.maximum(over_ref[...], other_over_ref[...])
    sent[OVER : OVER + 8, :] = over
    sent[4 * KINDS : 5 * KINDS, :] = to_owners(middle_ref[1], numbers_of(z1))
    for q, (rows, best) in enumerate(((own, near_ref[0]), (m1, near_ref[1]), (m3, near_ref[2]), (m2, middle_ref[0]))):
        best = all_earlier(best, rows, (z2,), order_ref, 0)
        sent[q * KINDS : (q + 1) * KINDS, :] = to_owners(best, numbers_of(rows))
    out_ref[...] = jnp.broadcast_to(over[0:1, :], (512, 128))
    to_x = jnp.where(lax.axis_index("core") == 0, lax.axis_index("x"), lax.axis_index("y"))
    out_ref[pl.ds(pl.multiple_of(to_x * 128, 128), 128), :] = jnp.transpose(sent[...])


def final_kernel(in_ref, out_ref, over_ref, picked):
    my_x, my_core = lax.axis_index("x"), lax.axis_index("core")
    over = jnp.where(iota((512, 128), 1) == OVER, in_ref[...], 0.0)
    over_ref[0, 0] = (jnp.max(over) > 0.5).astype(I32)
    first = jnp.where(my_core == 0, my_x * 128, my_x * 8)
    step = jnp.where(my_core == 0, 8, 128)
    for z in range(4):
        for r in range(4):
            at = pl.multiple_of(first + z * 32 + r * step, 8)
            picked[(z * 4 + r) * 8 : (z * 4 + r) * 8 + 8, :] = in_ref[pl.ds(at, 8), :]
    got = jnp.transpose(picked[...])
    lane = iota((KINDS, 128), 1) % 32
    best = got[0:KINDS, :]
    for q, away in ((1, 3), (2, 1), (3, 2)):
        part = got[q * KINDS : (q + 1) * KINDS, :]
        moved = jnp.where(
            lane >= 8 * away,
            pltpu.roll(part, 8 * away, 1),
            pltpu.roll(part, 128 + 8 * away - 32, 1),
        )
        best = jnp.maximum(best, moved)
    part = got[4 * KINDS : 5 * KINDS, :]
    best = jnp.maximum(best, jnp.where(my_core == 0, pltpu.roll(part, 32, 1), pltpu.roll(part, 96, 1)))
    shift = lane // 8 - iota((KINDS, 128), 0) // 2
    turned = best
    for d in (-3, -2, -1, 1, 2, 3):
        moved = pltpu.roll(pltpu.roll(best, (8 - 2 * d) % 8, 0), (8 * d) % 128, 1)
        turned = jnp.where(shift == d, moved, turned)
    out_ref[...] = jnp.where(my_core == 0, best, turned)


def call(kernel, out, scratch=(), ins=None, outs=None, cost=None):
    more = {}
    if ins is not None:
        more["in_specs"] = ins
    if outs is not None:
        more["out_specs"] = outs
    return pl.pallas_call(
        kernel,
        out_shape=out,
        scratch_shapes=list(scratch),
        cost_estimate=cost,
        compiler_params=pltpu.CompilerParams(vmem_limit_bytes=VMEM),
        **more,
    )


def move(a, to):
    at = lambda x, c, z, y: ((x % 4 * 2 + c) * 4 + z % 4) * 4 + y % 4
    places = [(x, c, z, y) for x in range(4) for c in range(2) for z in range(4) for y in range(4)]
    return lax.ppermute(a, AXES, [(at(*p), at(*to(*p))) for p in places])


def across(a, step):
    return move(a, lambda x, c, z, y: (x + (1 - c) * step, c, z, y + c * step))


def along(a, step):
    return move(a, lambda x, c, z, y: (x + c * step, c, z, y + (1 - c) * step))


def down(a):
    return move(a, lambda x, c, z, y: (x, c, z - 1 + 2 * c, y))


def core_swap(a):
    return lax.ppermute(a, "core", [(0, 1), (1, 0)])


def fast(embeddings, cluster_id, row_order, assignment, placement):
    vmem = pl.BlockSpec(memory_space=pltpu.VMEM)
    smem = pl.BlockSpec(memory_space=pltpu.SMEM)
    line = lambda a: a.reshape(1, ROWS)
    cheap = pl.CostEstimate(flops=10**9, bytes_accessed=2 * 10**6, transcendentals=0)
    blocks = jax.ShapeDtypeStruct((4 * BLOCK, WIDTH), BF16)
    same, other = call(
        prep_kernel,
        (blocks, blocks),
        ins=[smem] + [vmem] * 4,
        cost=cheap,
    )(assignment, embeddings, line(cluster_id), line(row_order), line(placement))
    other = core_swap(other)
    shape = (4, 1, BLOCK, WIDTH)
    both = jnp.concatenate([same.reshape(shape), other.reshape(shape)], axis=1).reshape(4, 2 * BLOCK, WIDTH)
    own, over = call(
        pack_kernel,
        (jax.ShapeDtypeStruct((PACKED, WIDTH), BF16), jax.ShapeDtypeStruct((8, 128), F32)),
        [pltpu.VMEM((KINDS * BLOCK, WIDTH), BF16)],
        cost=cheap,
    )(both[0], *[across(both[k], k) for k in (1, 2, 3)])
    half = PACKED // 2
    z1, m1, m3 = down(own), along(own, 1), along(own, -1)
    other_over = core_swap(over)
    z2, m2a, m2b = down(z1), along(m1[:half], 1), along(m3[half:], -1)
    product = 2 * PACKED * PACKED * WIDTH
    cost = lambda n: pl.CostEstimate(flops=n * product, bytes_accessed=6 * 10**6, transcendentals=0)
    order = pltpu.VMEM((PACKED, 8), F32)
    near = call(near_kernel, jax.ShapeDtypeStruct((4, 8, PACKED), F32), [order], cost=cost(9))(own, m1, m3, z1)
    m2, middle = call(
        middle_kernel,
        (jax.ShapeDtypeStruct((PACKED, WIDTH), BF16), jax.ShapeDtypeStruct((2, 8, PACKED), F32)),
        [order],
        cost=cost(3),
    )(own, z1, m2a, m2b, near)
    back = call(
        far_kernel,
        jax.ShapeDtypeStruct((512, 128), F32),
        [order, pltpu.VMEM((128, 128), F32)],
        cost=cost(4),
    )(own, m1, m3, m2, z1, z2, near, middle, over, other_over)
    back = lax.all_to_all(back, ("x", "z", "y"), split_axis=0, concat_axis=0, tiled=True)
    best, over = call(
        final_kernel,
        (jax.ShapeDtypeStruct((KINDS, 128), F32), jax.ShapeDtypeStruct((1, 1), I32)),
        [pltpu.VMEM((128, 128), F32)],
        ins=[vmem],
        outs=(vmem, smem),
    )(back)
    return best.reshape(KINDS * 128), over[0, 0] > 0


def slow(embeddings, cluster_id, row_order, assignment, placement):
    owners = KINDS * MEMBERS
    slots = owners * CAP
    wide = embeddings.astype(F32)
    mean = jnp.mean(wide * wide, axis=1, keepdims=True)
    unit = (wide * lax.rsqrt(mean + 1e-06) * (1.0 / math.sqrt(WIDTH))).astype(BF16)
    owner = jnp.sum(
        jnp.where(cluster_id[:, None] == jnp.arange(KINDS, dtype=I32)[None, :], assignment[None, :], 0), axis=1
    ) * MEMBERS + placement
    ids = jnp.arange(ROWS, dtype=I32)
    rank = jnp.sum(((owner[:, None] == owner[None, :]) & (ids[None, :] < ids[:, None])).astype(I32), axis=1)
    target = owner * CAP + rank
    units = jnp.zeros((slots, WIDTH), BF16).at[target].set(unit)
    orders = jnp.full((slots,), ROWS * owners, I32).at[target].set(row_order)
    swap = lambda a: lax.all_to_all(a, AXES, split_axis=0, concat_axis=0, tiled=True)
    units, orders = swap(units), swap(orders)

    def step(_, carried):
        best, piece, piece_orders = carried

        def block(packed):
            block_units, block_orders = packed
            scores = jnp.einsum("ik,jk->ij", block_units, piece, preferred_element_type=F32)
            fit = piece_orders[None, :] < block_orders[:, None]
            return jnp.max(jnp.where(fit, scores, -2.0), axis=1)

        here = lax.map(block, (units.reshape(2, slots // 2, WIDTH), orders.reshape(2, slots // 2)))
        best = jnp.maximum(best, here.reshape(slots))
        turn = [(i, (i + 1) % MEMBERS) for i in range(MEMBERS)]
        return best, lax.ppermute(piece, ("z", "y"), turn), lax.ppermute(piece_orders, ("z", "y"), turn)

    best = lax.fori_loop(0, MEMBERS, step, (jnp.full((slots,), -2.0, F32), units, orders))[0]
    return jnp.where(orders < ROWS * owners, jnp.maximum(best, -1.0), -1.0)


def local(*args):
    best, over = fast(*args)
    return lax.cond(over, lambda args, best: slow(*args), lambda args, best: best, args, best)


def solution(mesh):
    fine = Mesh(mesh.devices.reshape(4, 2, 4, 4), AXES)
    return jax.shard_map(
        local,
        mesh=fine,
        in_specs=(P(AXES, None), P(AXES), P(AXES), P(), P(AXES)),
        out_specs=P(AXES),
        check_vma=False,
    )
```

```python
import math

import jax
import jax.numpy as jnp
from jax import lax
from jax.experimental import pallas as pl
from jax.experimental.pallas import tpu as pltpu
from jax.sharding import Mesh
from jax.sharding import PartitionSpec as P

F32, BF16, I32 = jnp.float32, jnp.bfloat16, jnp.int32
AXES = ("x", "core", "z", "y")
WIDTH = 768
ROWS = 512
KINDS = 8
MEMBERS = 16
CAP = 8
SEND = 96
BLOCK = SEND + 8
PACKED = 640
HEAD = 16
HELD = PACKED - HEAD
HALF = PACKED // 2
FAR = 256.0
VMEM = 16 * 2**20


def iota(shape, axis):
    return lax.broadcasted_iota(I32, shape, axis)


def iota_f(shape, axis):
    return iota(shape, axis).astype(F32)


def hot(hits):
    return jnp.where(hits, 1.0, 0.0).astype(BF16)


def mul(a, b):
    return jnp.dot(a, b, preferred_element_type=F32)


def mul_nt(a, b):
    return lax.dot_general(a, b, (((1,), (1,)), ((), ())), preferred_element_type=F32)


def rows_of(*rows):
    n = next(r.shape[1] for r in rows if r is not None)
    at = iota((8, n), 0)
    out = jnp.zeros((8, n), F32)
    for i, row in enumerate(rows):
        if row is not None:
            out = jnp.where(at == i, jnp.broadcast_to(row, (8, n)), out)
    return out


def prep_kernel(assign_ref, emb_ref, cid_ref, order_ref, place_ref, other_ref, both_ref, target_ref):
    wide = emb_ref[...].astype(F32)
    mean = jnp.mean(wide * wide, axis=1, keepdims=True)
    unit = (wide * lax.rsqrt(mean + 1e-06) * (1.0 / math.sqrt(WIDTH))).astype(BF16)
    my_x, my_core, my_y = lax.axis_index("x"), lax.axis_index("core"), lax.axis_index("y")
    cid = cid_ref[...]
    group = jnp.zeros_like(cid)
    for c in range(KINDS):
        core = lax.rem(assign_ref[c], 2)
        away = lax.rem(assign_ref[c] // 2 - jnp.where(core == 0, my_x, my_y) + 4, 4)
        away += 4 * lax.rem(core + my_core, 2)
        group = jnp.where(cid == c, away, group)
    group = group.astype(F32)
    place = place_ref[...].astype(F32)
    owner = group * MEMBERS + place
    columns = jnp.transpose(rows_of(group, owner))
    before = iota((ROWS, ROWS), 0) < iota((ROWS, ROWS), 1)

    def rank(column, row):
        return jnp.sum(jnp.where(before & (column == row), 1.0, 0.0), axis=0, keepdims=True)

    in_group = rank(columns[:, 0:1], group)
    in_owner = rank(columns[:, 1:2], owner)
    fits = in_group < SEND
    order = order_ref[...]
    high = (order // 256).astype(F32)
    low = (order % 256).astype(F32)
    kind = jnp.where(iota_f((KINDS, ROWS), 0) == group, 1.0, 0.0)
    numbers = jnp.concatenate([kind * high, kind * low, kind * (place * CAP + in_owner + 1.0)], axis=0)
    slot = jnp.transpose(rows_of(in_group))[:, 0:1]
    spread = mul(numbers.astype(BF16), hot(iota_f((ROWS, 128), 1) == slot))
    spread = jnp.where(iota((24, 128), 1) < SEND, spread, 0.0)
    counts = jnp.zeros((KINDS, 128), F32)
    for c in range(KINDS):
        count = jnp.sum(jnp.where(cid == c, 1.0, 0.0), axis=1, keepdims=True)
        counts = jnp.where(iota((KINDS, 128), 1) == assign_ref[c], count, counts)
    numbers = jnp.concatenate([spread, counts, jnp.zeros((96, 128), F32)], axis=0)
    numbers = jnp.concatenate([numbers, jnp.zeros((128, WIDTH - 128), F32)], axis=1).astype(BF16)
    at = iota((1, 128), 1)
    at = jnp.where(at < 32, (at % 8) * BLOCK + SEND + at // 8, -1).astype(F32)
    target = jnp.concatenate([jnp.where(fits, group * BLOCK + in_group, -1.0), at], axis=1)
    both = jnp.concatenate([unit, numbers], axis=0)
    both_ref[...] = both
    target_ref[...] = jnp.broadcast_to(target, (8, ROWS + 128))
    half = 4 * BLOCK
    placing = hot(iota_f((half, ROWS + 128), 0) == target - half)
    other_ref[...] = mul(placing, both).astype(BF16)


def same_kernel(both_ref, target_ref, same_ref):
    placing = hot(iota_f((4 * BLOCK, ROWS + 128), 0) == target_ref[0:1, :])
    same_ref[...] = mul(placing, both_ref[...]).astype(BF16)


def pack_kernel(here_ref, from1_ref, from2_ref, from3_ref, out_ref, low_ref, high_ref, over_ref, in_ref):
    count = KINDS * BLOCK
    for k, ref in enumerate((here_ref, from1_ref, from2_ref, from3_ref)):
        in_ref[k * 2 * BLOCK : (k + 1) * 2 * BLOCK, :] = ref[...]
    my_core = lax.axis_index("core")
    my_line = jnp.where(my_core == 0, lax.axis_index("x"), lax.axis_index("y"))
    at = iota((32, count), 0)
    pick = hot(iota((32, count), 1) == (at % 8) * BLOCK + SEND + at // 8)
    numbers = mul(pick, in_ref[:, 0:128])
    n = jnp.sum(jnp.where(numbers[16:24, :] > 0.0, 1.0, 0.0), axis=1, keepdims=True)
    line = iota((KINDS, 1), 0)
    base = jnp.zeros((KINDS, 1), F32)
    source = jnp.zeros((KINDS, 1), F32)
    lane = iota_f((1, count), 1)
    position = jnp.full((1, count), -1.0, F32)
    start = jnp.full((1, 1), float(HEAD), F32)
    for b in range(KINDS):
        step = lane - b * BLOCK
        mine = n[b : b + 1, :]
        position = jnp.where((step >= 0.0) & (step < mine), start + step, position)
        base = jnp.where(line == b, start, base)
        from_device = 2 * lax.rem(my_line - b // 2 + 4, 4) + lax.rem(my_core + b % 2, 2)
        source = jnp.where(line == b, from_device.astype(F32), source)
        start = start + mine
    position = jnp.where(position < PACKED, position, -1.0)
    placing = hot(iota_f((HELD, count), 0) == position - HEAD)
    out_ref[HEAD:PACKED, :] = mul(placing, in_ref[...]).astype(BF16)
    step = iota_f((KINDS, PACKED), 1) - base
    mine = jnp.where((step >= 0.0) & (step < n), 1.0, 0.0)
    slot = jnp.sum(mine * step, axis=0, keepdims=True)
    found = mul(numbers[0:24, :].astype(BF16), hot(iota_f((128, PACKED), 0) == slot))
    high, low, code = (
        jnp.sum(mine * found[i * 8 : i * 8 + 8, :], axis=0, keepdims=True) for i in range(3)
    )
    source = jnp.sum(mine * source, axis=0, keepdims=True)
    counts = numbers[24:32, :]
    over = jnp.max(jnp.where(counts > SEND, 1.0, 0.0), axis=0, keepdims=True)
    ours = iota((1, 128), 1) % 2 == my_core
    full = ours & (jnp.sum(counts, axis=0, keepdims=True) > HELD)
    over = jnp.maximum(over, jnp.where(full, 1.0, 0.0))
    over = jnp.max(over, axis=1, keepdims=True)
    valid = code > 0.0
    final = rows_of(
        jnp.where(valid, high, FAR),
        jnp.where(valid, low, 0.0),
        jnp.where(valid, code, 0.0),
        jnp.where(valid, source, 0.0),
    )
    over_ref[...] = jnp.broadcast_to(over, (8, 128))
    final = jnp.concatenate([final, jnp.zeros((8, WIDTH - PACKED), F32)], axis=1)
    final = jnp.concatenate([final, jnp.zeros((8, WIDTH), F32)], axis=0)
    out_ref[0:HEAD, :] = final.astype(BF16)
    low_ref[...] = out_ref[0:HALF, :]
    high_ref[...] = out_ref[HALF:PACKED, :]


def numbers_of(ref):
    return ref[0:HEAD, :].astype(F32)[0:8, 0:PACKED]


def orders_of(numbers):
    return numbers[0:1, :] * 256.0 + numbers[1:2, :]


def earlier_max(best, rows_ref, row_order, cols_ref, col_order):
    scores = mul_nt(cols_ref[...], rows_ref[...])
    scores = jnp.where(col_order < row_order, scores, -2.0)
    count, n = scores.shape
    return jnp.maximum(best, jnp.max(scores.reshape(count // 8, 8, n), axis=0))


def orders_down(*refs):
    return jnp.transpose(rows_of(*[orders_of(numbers_of(r)) for r in refs]))


def all_earlier(best, rows, cols, orders, first):
    order = orders_of(numbers_of(rows))
    for k, col in enumerate(cols):
        best = earlier_max(best, rows, order, col, orders[:, first + k : first + k + 1])
    return best


def nothing():
    return jnp.full((8, PACKED), -2.0, F32)


def owner_lines(numbers, lines_ref, hot_ref, q):
    lines_ref[q] = jnp.where((iota_f((KINDS, PACKED), 0) == numbers[3:4, :]) & (numbers[2:3, :] > 0.0), 1.0, 0.0)
    code = jnp.transpose(rows_of(numbers[2:3, :]))[:, 0:1]
    hot_ref[q] = hot(iota_f((PACKED, 128), 1) == code - 1.0)


def half_earlier(best, rows, half, order):
    return earlier_max(best, rows, orders_of(numbers_of(rows)), half, order)


def first_kernel(own, z1a, z1b, z1, best_ref, lines_ref, hot_ref, order_ref):
    z1[0:HALF, :] = z1a[...]
    z1[HALF:PACKED, :] = z1b[...]
    order_ref[...] = orders_down(z1, own)
    best_ref[0] = all_earlier(nothing(), own, (z1, own), order_ref, 0)
    best_ref[1] = all_earlier(nothing(), z1, (own,), order_ref, 1)
    owner_lines(numbers_of(own), lines_ref, hot_ref, 0)
    owner_lines(numbers_of(z1), lines_ref, hot_ref, 1)


def near_kernel(own, m1, m3, z1, z2a, first_ref, best_ref, lines_ref, hot_ref, order_ref):
    order_ref[...] = orders_down(z1, own, m1, m3, z2a)
    there = order_ref[0:HALF, 4:5]
    best_ref[2] = all_earlier(first_ref[1], z1, (m1, m3), order_ref, 2)
    best_ref[0] = half_earlier(all_earlier(nothing(), m1, (z1, own), order_ref, 0), m1, z2a, there)
    best_ref[1] = half_earlier(all_earlier(nothing(), m3, (z1, own), order_ref, 0), m3, z2a, there)
    best_ref[3] = half_earlier(first_ref[0], own, z2a, there)
    owner_lines(numbers_of(m1), lines_ref, hot_ref, 0)
    owner_lines(numbers_of(m3), lines_ref, hot_ref, 1)


def middle_kernel(
    own, m2a, m2b, z1, z2a, near_ref, first_lines_ref, first_hot_ref, m2, best_ref, sent_ref, lines_ref, hot_ref, order_ref
):
    m2[0:HALF, :] = m2a[...]
    m2[HALF:PACKED, :] = m2b[...]
    order_ref[...] = orders_down(z1, own, m2, z2a)
    best = all_earlier(near_ref[2], z1, (m2,), order_ref, 2)
    best_ref[0] = half_earlier(
        all_earlier(nothing(), m2, (z1, own), order_ref, 0), m2, z2a, order_ref[0:HALF, 3:4]
    )
    sent_ref[...] = to_owners(best, first_lines_ref[1], first_hot_ref[1])
    owner_lines(numbers_of(m2), lines_ref, hot_ref, 0)


def to_owners(best, lines, places):
    best = jnp.maximum(jnp.max(best, axis=0, keepdims=True), -1.0)
    high = best.astype(BF16).astype(F32)
    low = best - high
    middle = low.astype(BF16).astype(F32)
    low = low - middle
    pieces = jnp.concatenate([lines, lines * high, lines * middle, lines * low], axis=0)
    put = mul(pieces.astype(BF16), places)
    return (put[0:8, :] - 1.0) + (put[8:16, :] + put[16:24, :] + put[24:32, :])


OVER = 5 * KINDS


def far_kernel(
    own, m1, m3, m2, z2b, first_lines, first_hot, near_ref, near_lines, near_hot,
    middle_ref, middle_sent, middle_lines, middle_hot, orders, over_ref, other_over_ref, out_ref, sent,
):
    sent[...] = jnp.zeros((128, 128), F32)
    over = jnp.maximum(over_ref[...], other_over_ref[...])
    sent[OVER : OVER + 8, :] = over
    sent[3 * KINDS : 4 * KINDS, :] = middle_sent[...]
    there = orders[HALF:PACKED, 3:4]
    bests = [
        half_earlier(best, rows, z2b, there)
        for rows, best in ((own, near_ref[3]), (m1, near_ref[0]), (m3, near_ref[1]), (m2, middle_ref[0]))
    ]
    for q, best, lines, places in (
        (0, bests[0], first_lines[0], first_hot[0]),
        (1, bests[1], near_lines[0], near_hot[0]),
        (2, bests[2], near_lines[1], near_hot[1]),
        (4, bests[3], middle_lines[0], middle_hot[0]),
    ):
        sent[q * KINDS : (q + 1) * KINDS, :] = to_owners(best, lines, places)
    out_ref[...] = jnp.broadcast_to(over[0:1, :], (512, 128))
    to_x = jnp.where(lax.axis_index("core") == 0, lax.axis_index("x"), lax.axis_index("y"))
    out_ref[pl.ds(pl.multiple_of(to_x * 128, 128), 128), :] = jnp.transpose(sent[...])


def final_kernel(in_ref, out_ref, over_ref, picked):
    my_x, my_core = lax.axis_index("x"), lax.axis_index("core")
    over = jnp.where(iota((512, 128), 1) == OVER, in_ref[...], 0.0)
    over_ref[0, 0] = (jnp.max(over) > 0.5).astype(I32)
    first = jnp.where(my_core == 0, my_x * 128, my_x * 8)
    step = jnp.where(my_core == 0, 8, 128)
    for z in range(4):
        for r in range(4):
            at = pl.multiple_of(first + z * 32 + r * step, 8)
            picked[(z * 4 + r) * 8 : (z * 4 + r) * 8 + 8, :] = in_ref[pl.ds(at, 8), :]
    got = jnp.transpose(picked[...])
    lane = iota((KINDS, 128), 1) % 32
    best = got[0:KINDS, :]
    for q, away in ((1, 3), (2, 1), (4, 2)):
        part = got[q * KINDS : (q + 1) * KINDS, :]
        moved = jnp.where(
            lane >= 8 * away,
            pltpu.roll(part, 8 * away, 1),
            pltpu.roll(part, 128 + 8 * away - 32, 1),
        )
        best = jnp.maximum(best, moved)
    part = got[3 * KINDS : 4 * KINDS, :]
    best = jnp.maximum(best, jnp.where(my_core == 0, pltpu.roll(part, 32, 1), pltpu.roll(part, 96, 1)))
    shift = lane // 8 - iota((KINDS, 128), 0) // 2
    turned = best
    for d in (-3, -2, -1, 1, 2, 3):
        moved = pltpu.roll(pltpu.roll(best, (8 - 2 * d) % 8, 0), (8 * d) % 128, 1)
        turned = jnp.where(shift == d, moved, turned)
    out_ref[...] = jnp.where(my_core == 0, best, turned)


def call(kernel, out, scratch=(), ins=None, outs=None, cost=None):
    more = {}
    if ins is not None:
        more["in_specs"] = ins
    if outs is not None:
        more["out_specs"] = outs
    return pl.pallas_call(
        kernel,
        out_shape=out,
        scratch_shapes=list(scratch),
        cost_estimate=cost,
        compiler_params=pltpu.CompilerParams(vmem_limit_bytes=VMEM),
        **more,
    )


def move(a, to):
    at = lambda x, c, z, y: ((x % 4 * 2 + c) * 4 + z % 4) * 4 + y % 4
    places = [(x, c, z, y) for x in range(4) for c in range(2) for z in range(4) for y in range(4)]
    return lax.ppermute(a, AXES, [(at(*p), at(*to(*p))) for p in places])


def across(a, step):
    return move(a, lambda x, c, z, y: (x + (1 - c) * step, c, z, y + c * step))


def along(a, step):
    return move(a, lambda x, c, z, y: (x + c * step, c, z, y + (1 - c) * step))


def down(a):
    return move(a, lambda x, c, z, y: (x, c, z - 1 + 2 * c, y))


def core_swap(a):
    return lax.ppermute(a, "core", [(0, 1), (1, 0)])


def fast(embeddings, cluster_id, row_order, assignment, placement):
    vmem = pl.BlockSpec(memory_space=pltpu.VMEM)
    smem = pl.BlockSpec(memory_space=pltpu.SMEM)
    line = lambda a: a.reshape(1, ROWS)
    cheap = pl.CostEstimate(flops=10**9, bytes_accessed=2 * 10**6, transcendentals=0)
    blocks = jax.ShapeDtypeStruct((4 * BLOCK, WIDTH), BF16)
    other, pool, target = call(
        prep_kernel,
        (
            blocks,
            jax.ShapeDtypeStruct((ROWS + 128, WIDTH), BF16),
            jax.ShapeDtypeStruct((8, ROWS + 128), F32),
        ),
        ins=[smem] + [vmem] * 4,
        cost=cheap,
    )(assignment, embeddings, line(cluster_id), line(row_order), line(placement))
    other = core_swap(other)
    same = call(same_kernel, blocks, cost=cheap)(pool, target)
    shape = (4, 1, BLOCK, WIDTH)
    both = jnp.concatenate([same.reshape(shape), other.reshape(shape)], axis=1).reshape(4, 2 * BLOCK, WIDTH)
    piece = jax.ShapeDtypeStruct((HALF, WIDTH), BF16)
    part = jax.ShapeDtypeStruct((PACKED, WIDTH), BF16)
    own, low, high, over = call(
        pack_kernel,
        (part, piece, piece, jax.ShapeDtypeStruct((8, 128), F32)),
        [pltpu.VMEM((KINDS * BLOCK, WIDTH), BF16)],
        cost=cheap,
    )(both[0], *[across(both[k], k) for k in (1, 2, 3)])
    z1a, z1b = down(low), down(high)
    m1, m3 = along(own, 1), along(own, -1)
    other_over = core_swap(over)
    z2a, z2b = down(z1a), down(z1b)
    m2a, m2b = along(m1[:HALF], 1), along(m3[HALF:], -1)
    product = 2 * PACKED * PACKED * WIDTH
    cost = lambda n: pl.CostEstimate(flops=n * product, bytes_accessed=6 * 10**6, transcendentals=0)
    order = pltpu.VMEM((PACKED, 8), F32)
    made = lambda n, k: (
        jax.ShapeDtypeStruct((n, 8, PACKED), F32),
        jax.ShapeDtypeStruct((k, 8, PACKED), F32),
        jax.ShapeDtypeStruct((k, PACKED, 128), BF16),
    )
    z1, *first = call(first_kernel, (part, *made(2, 2)), [order], cost=cost(3))(own, z1a, z1b)
    near = call(near_kernel, made(4, 2), [order], cost=cost(7))(own, m1, m3, z1, z2a, first[0])
    best, lines, hots = made(1, 1)
    m2, *middle, orders = call(
        middle_kernel,
        (part, best, jax.ShapeDtypeStruct((8, 128), F32), lines, hots, jax.ShapeDtypeStruct((PACKED, 8), F32)),
        cost=cost(3),
    )(own, m2a, m2b, z1, z2a, near[0], *first[1:])
    back = call(
        far_kernel,
        jax.ShapeDtypeStruct((512, 128), F32),
        [pltpu.VMEM((128, 128), F32)],
        cost=cost(2),
    )(own, m1, m3, m2, z2b, *first[1:], *near, *middle, orders, over, other_over)
    back = lax.all_to_all(back, ("x", "z", "y"), split_axis=0, concat_axis=0, tiled=True)
    best, over = call(
        final_kernel,
        (jax.ShapeDtypeStruct((KINDS, 128), F32), jax.ShapeDtypeStruct((1, 1), I32)),
        [pltpu.VMEM((128, 128), F32)],
        ins=[vmem],
        outs=(vmem, smem),
    )(back)
    return best.reshape(KINDS * 128), over[0, 0] > 0


def slow(embeddings, cluster_id, row_order, assignment, placement):
    owners = KINDS * MEMBERS
    slots = owners * CAP
    wide = embeddings.astype(F32)
    mean = jnp.mean(wide * wide, axis=1, keepdims=True)
    unit = (wide * lax.rsqrt(mean + 1e-06) * (1.0 / math.sqrt(WIDTH))).astype(BF16)
    owner = jnp.sum(
        jnp.where(cluster_id[:, None] == jnp.arange(KINDS, dtype=I32)[None, :], assignment[None, :], 0), axis=1
    ) * MEMBERS + placement
    ids = jnp.arange(ROWS, dtype=I32)
    rank = jnp.sum(((owner[:, None] == owner[None, :]) & (ids[None, :] < ids[:, None])).astype(I32), axis=1)
    target = owner * CAP + rank
    units = jnp.zeros((slots, WIDTH), BF16).at[target].set(unit)
    orders = jnp.full((slots,), ROWS * owners, I32).at[target].set(row_order)
    swap = lambda a: lax.all_to_all(a, AXES, split_axis=0, concat_axis=0, tiled=True)
    units, orders = swap(units), swap(orders)

    def step(_, carried):
        best, piece, piece_orders = carried

        def block(packed):
            block_units, block_orders = packed
            scores = jnp.einsum("ik,jk->ij", block_units, piece, preferred_element_type=F32)
            fit = piece_orders[None, :] < block_orders[:, None]
            return jnp.max(jnp.where(fit, scores, -2.0), axis=1)

        here = lax.map(block, (units.reshape(2, slots // 2, WIDTH), orders.reshape(2, slots // 2)))
        best = jnp.maximum(best, here.reshape(slots))
        turn = [(i, (i + 1) % MEMBERS) for i in range(MEMBERS)]
        return best, lax.ppermute(piece, ("z", "y"), turn), lax.ppermute(piece_orders, ("z", "y"), turn)

    best = lax.fori_loop(0, MEMBERS, step, (jnp.full((slots,), -2.0, F32), units, orders))[0]
    return jnp.where(orders < ROWS * owners, jnp.maximum(best, -1.0), -1.0)


def local(*args):
    best, over = fast(*args)
    return lax.cond(over, lambda args, best: slow(*args), lambda args, best: best, args, best)


def solution(mesh):
    fine = Mesh(mesh.devices.reshape(4, 2, 4, 4), AXES)
    return jax.shard_map(
        local,
        mesh=fine,
        in_specs=(P(AXES, None), P(AXES), P(AXES), P(), P(AXES)),
        out_specs=P(AXES),
        check_vma=False,
    )
```

```python
import math

import jax
import jax.numpy as jnp
from jax import lax
from jax.experimental import pallas as pl
from jax.experimental.pallas import tpu as pltpu
from jax.sharding import Mesh
from jax.sharding import PartitionSpec as P

F32, BF16, I32 = jnp.float32, jnp.bfloat16, jnp.int32
AXES = ("x", "core", "z", "y")
WIDTH = 768
ROWS = 512
KINDS = 8
MEMBERS = 16
CAP = 8
SEND = 96
BLOCK = SEND + 8
PACKED = 640
HEAD = 16
HELD = PACKED - HEAD
HALF = PACKED // 2
FAR = 256.0
VMEM = 16 * 2**20


def iota(shape, axis):
    return lax.broadcasted_iota(I32, shape, axis)


def iota_f(shape, axis):
    return iota(shape, axis).astype(F32)


def hot(hits):
    return jnp.where(hits, 1.0, 0.0).astype(BF16)


def mul(a, b):
    return jnp.dot(a, b, preferred_element_type=F32)


def mul_nt(a, b):
    return lax.dot_general(a, b, (((1,), (1,)), ((), ())), preferred_element_type=F32)


def rows_of(*rows):
    n = next(r.shape[1] for r in rows if r is not None)
    at = iota((8, n), 0)
    out = jnp.zeros((8, n), F32)
    for i, row in enumerate(rows):
        if row is not None:
            out = jnp.where(at == i, jnp.broadcast_to(row, (8, n)), out)
    return out


def prep_kernel(assign_ref, emb_ref, cid_ref, order_ref, place_ref, other_ref, both_ref, target_ref):
    wide = emb_ref[...].astype(F32)
    mean = jnp.mean(wide * wide, axis=1, keepdims=True)
    unit = (wide * lax.rsqrt(mean + 1e-06) * (1.0 / math.sqrt(WIDTH))).astype(BF16)
    my_x, my_core, my_y = lax.axis_index("x"), lax.axis_index("core"), lax.axis_index("y")
    cid = cid_ref[...]
    group = jnp.zeros_like(cid)
    for c in range(KINDS):
        core = lax.rem(assign_ref[c], 2)
        away = lax.rem(assign_ref[c] // 2 - jnp.where(core == 0, my_x, my_y) + 4, 4)
        away += 4 * lax.rem(core + my_core, 2)
        group = jnp.where(cid == c, away, group)
    group = group.astype(F32)
    place = place_ref[...].astype(F32)
    owner = group * MEMBERS + place
    columns = jnp.transpose(rows_of(group, owner))
    before = iota((ROWS, ROWS), 0) < iota((ROWS, ROWS), 1)

    def rank(column, row):
        return jnp.sum(jnp.where(before & (column == row), 1.0, 0.0), axis=0, keepdims=True)

    in_group = rank(columns[:, 0:1], group)
    in_owner = rank(columns[:, 1:2], owner)
    fits = in_group < SEND
    order = order_ref[...]
    high = (order // 256).astype(F32)
    low = (order % 256).astype(F32)
    kind = jnp.where(iota_f((KINDS, ROWS), 0) == group, 1.0, 0.0)
    numbers = jnp.concatenate([kind * high, kind * low, kind * (place * CAP + in_owner + 1.0)], axis=0)
    slot = jnp.transpose(rows_of(in_group))[:, 0:1]
    spread = mul(numbers.astype(BF16), hot(iota_f((ROWS, 128), 1) == slot))
    spread = jnp.where(iota((24, 128), 1) < SEND, spread, 0.0)
    counts = jnp.zeros((KINDS, 128), F32)
    for c in range(KINDS):
        count = jnp.sum(jnp.where(cid == c, 1.0, 0.0), axis=1, keepdims=True)
        counts = jnp.where(iota((KINDS, 128), 1) == assign_ref[c], count, counts)
    numbers = jnp.concatenate([spread, counts, jnp.zeros((96, 128), F32)], axis=0)
    numbers = jnp.concatenate([numbers, jnp.zeros((128, WIDTH - 128), F32)], axis=1).astype(BF16)
    at = iota((1, 128), 1)
    at = jnp.where(at < 32, (at % 8) * BLOCK + SEND + at // 8, -1).astype(F32)
    target = jnp.concatenate([jnp.where(fits, group * BLOCK + in_group, -1.0), at], axis=1)
    both = jnp.concatenate([unit, numbers], axis=0)
    both_ref[...] = both
    target_ref[...] = jnp.broadcast_to(target, (8, ROWS + 128))
    half = 4 * BLOCK
    placing = hot(iota_f((half, ROWS + 128), 0) == target - half)
    other_ref[...] = mul(placing, both).astype(BF16)


def same_kernel(both_ref, target_ref, same_ref):
    placing = hot(iota_f((4 * BLOCK, ROWS + 128), 0) == target_ref[0:1, :])
    same_ref[...] = mul(placing, both_ref[...]).astype(BF16)


def pack_kernel(here_ref, from1_ref, from2_ref, from3_ref, out_ref, low_ref, high_ref, over_ref, in_ref):
    count = KINDS * BLOCK
    for k, ref in enumerate((here_ref, from1_ref, from2_ref, from3_ref)):
        in_ref[k * 2 * BLOCK : (k + 1) * 2 * BLOCK, :] = ref[...]
    my_core = lax.axis_index("core")
    my_line = jnp.where(my_core == 0, lax.axis_index("x"), lax.axis_index("y"))
    at = iota((32, count), 0)
    pick = hot(iota((32, count), 1) == (at % 8) * BLOCK + SEND + at // 8)
    numbers = mul(pick, in_ref[:, 0:128])
    n = jnp.sum(jnp.where(numbers[16:24, :] > 0.0, 1.0, 0.0), axis=1, keepdims=True)
    line = iota((KINDS, 1), 0)
    base = jnp.zeros((KINDS, 1), F32)
    source = jnp.zeros((KINDS, 1), F32)
    lane = iota_f((1, count), 1)
    position = jnp.full((1, count), -1.0, F32)
    start = jnp.full((1, 1), float(HEAD), F32)
    for b in range(KINDS):
        step = lane - b * BLOCK
        mine = n[b : b + 1, :]
        position = jnp.where((step >= 0.0) & (step < mine), start + step, position)
        base = jnp.where(line == b, start, base)
        from_device = 2 * lax.rem(my_line - b // 2 + 4, 4) + lax.rem(my_core + b % 2, 2)
        source = jnp.where(line == b, from_device.astype(F32), source)
        start = start + mine
    position = jnp.where(position < PACKED, position, -1.0)
    placing = hot(iota_f((HELD, count), 0) == position - HEAD)
    out_ref[HEAD:PACKED, :] = mul(placing, in_ref[...]).astype(BF16)
    step = iota_f((KINDS, PACKED), 1) - base
    mine = jnp.where((step >= 0.0) & (step < n), 1.0, 0.0)
    slot = jnp.sum(mine * step, axis=0, keepdims=True)
    found = mul(numbers[0:24, :].astype(BF16), hot(iota_f((128, PACKED), 0) == slot))
    high, low, code = (
        jnp.sum(mine * found[i * 8 : i * 8 + 8, :], axis=0, keepdims=True) for i in range(3)
    )
    source = jnp.sum(mine * source, axis=0, keepdims=True)
    counts = numbers[24:32, :]
    over = jnp.max(jnp.where(counts > SEND, 1.0, 0.0), axis=0, keepdims=True)
    ours = iota((1, 128), 1) % 2 == my_core
    full = ours & (jnp.sum(counts, axis=0, keepdims=True) > HELD)
    over = jnp.maximum(over, jnp.where(full, 1.0, 0.0))
    over = jnp.max(over, axis=1, keepdims=True)
    valid = code > 0.0
    final = rows_of(
        jnp.where(valid, high, FAR),
        jnp.where(valid, low, 0.0),
        jnp.where(valid, code, 0.0),
        jnp.where(valid, source, 0.0),
    )
    over_ref[...] = jnp.broadcast_to(over, (8, 128))
    final = jnp.concatenate([final, jnp.zeros((8, WIDTH - PACKED), F32)], axis=1)
    final = jnp.concatenate([final, jnp.zeros((8, WIDTH), F32)], axis=0)
    out_ref[0:HEAD, :] = final.astype(BF16)
    low_ref[...] = out_ref[0:HALF, :]
    high_ref[...] = out_ref[HALF:PACKED, :]


def numbers_of(ref):
    return ref[0:HEAD, :].astype(F32)[0:8, 0:PACKED]


def orders_of(numbers):
    return numbers[0:1, :] * 256.0 + numbers[1:2, :]


def earlier_max(best, rows_ref, row_order, cols_ref, col_order):
    scores = mul_nt(cols_ref[...], rows_ref[...])
    scores = jnp.where(col_order < row_order, scores, -2.0)
    count, n = scores.shape
    return jnp.maximum(best, jnp.max(scores.reshape(count // 8, 8, n), axis=0))


def orders_down(*refs):
    return jnp.transpose(rows_of(*[orders_of(numbers_of(r)) for r in refs]))


def all_earlier(best, rows, cols, orders, first):
    order = orders_of(numbers_of(rows))
    for k, col in enumerate(cols):
        best = earlier_max(best, rows, order, col, orders[:, first + k : first + k + 1])
    return best


def nothing():
    return jnp.full((8, PACKED), -2.0, F32)


def owner_lines(numbers, lines_ref, hot_ref, q):
    lines_ref[q] = jnp.where((iota_f((KINDS, PACKED), 0) == numbers[3:4, :]) & (numbers[2:3, :] > 0.0), 1.0, 0.0)
    code = jnp.transpose(rows_of(numbers[2:3, :]))[:, 0:1]
    hot_ref[q] = hot(iota_f((PACKED, 128), 1) == code - 1.0)


def half_earlier(best, rows, half, order):
    return earlier_max(best, rows, orders_of(numbers_of(rows)), half, order)


def both_ways(best, far_best, rows, z1, z1_order):
    scores = mul_nt(z1[...], rows[...])
    earlier = z1_order < orders_of(numbers_of(rows))
    count, n = scores.shape
    ours = jnp.where(earlier, scores, -2.0)
    theirs = jnp.where(earlier, -2.0, scores)
    for k in range(n // 128):
        far_best = jnp.maximum(far_best, theirs[:, k * 128 : (k + 1) * 128])
    return jnp.maximum(best, jnp.max(ours.reshape(count // 8, 8, n), axis=0)), far_best


def own_kernel(own, best_ref, lines_ref, hot_ref, order_ref):
    order_ref[...] = orders_down(own)
    best_ref[0] = all_earlier(nothing(), own, (own,), order_ref, 0)
    owner_lines(numbers_of(own), lines_ref, hot_ref, 0)


def ring_kernel(own, m1, m3, over_a, over_b, best_ref, lines_ref, hot_ref, over_ref, order_ref):
    order_ref[...] = orders_down(own)
    for i, rows in enumerate((m1, m3)):
        best_ref[i] = all_earlier(nothing(), rows, (own,), order_ref, 0)
        owner_lines(numbers_of(rows), lines_ref, hot_ref, i)
    over_ref[...] = jnp.maximum(over_a[...], over_b[...])


def near_kernel(own, m1, m3, z1a, z1b, z2a, own_ref, ring_ref, z1, best_ref, far_best_ref, lines_ref, hot_ref, order_ref):
    z1[0:HALF, :] = z1a[...]
    z1[HALF:PACKED, :] = z1b[...]
    order_ref[...] = orders_down(z1, z2a)
    far_best = jnp.full((PACKED, 128), -2.0, F32)
    for i, (rows, best) in enumerate(((own, own_ref[0]), (m1, ring_ref[0]), (m3, ring_ref[1]))):
        best, far_best = both_ways(best, far_best, rows, z1, order_ref[:, 0:1])
        best_ref[i] = half_earlier(best, rows, z2a, order_ref[0:HALF, 1:2])
    far_best_ref[...] = far_best
    owner_lines(numbers_of(z1), lines_ref, hot_ref, 0)


def middle_kernel(
    own, m2a, m2b, z1, z2a, far_best_ref, z1_lines, z1_hot, m2, best_ref, sent_ref, lines_ref, hot_ref, order_ref
):
    m2[0:HALF, :] = m2a[...]
    m2[HALF:PACKED, :] = m2b[...]
    order_ref[...] = orders_down(z1, own, z2a)
    best, far_best = both_ways(nothing(), far_best_ref[...], m2, z1, order_ref[:, 0:1])
    far_best = jnp.max(far_best, axis=1, keepdims=True)
    far_best = jnp.transpose(jnp.broadcast_to(far_best, (PACKED, 8)))
    best = all_earlier(best, m2, (own,), order_ref, 1)
    best_ref[0] = half_earlier(best, m2, z2a, order_ref[0:HALF, 2:3])
    sent_ref[...] = to_owners(far_best, z1_lines[0], z1_hot[0])
    owner_lines(numbers_of(m2), lines_ref, hot_ref, 0)


def to_owners(best, lines, places):
    best = jnp.maximum(jnp.max(best, axis=0, keepdims=True), -1.0)
    high = best.astype(BF16).astype(F32)
    low = best - high
    middle = low.astype(BF16).astype(F32)
    low = low - middle
    pieces = jnp.concatenate([lines, lines * high, lines * middle, lines * low], axis=0)
    put = mul(pieces.astype(BF16), places)
    return (put[0:8, :] - 1.0) + (put[8:16, :] + put[16:24, :] + put[24:32, :])


OVER = 5 * KINDS


def far_kernel(
    own, m1, m3, m2, z2b, own_lines, own_hot, ring_lines, ring_hot, near_ref,
    middle_ref, middle_sent, middle_lines, middle_hot, orders, over_ref, out_ref, sent,
):
    sent[...] = jnp.zeros((128, 128), F32)
    over = over_ref[...]
    sent[OVER : OVER + 8, :] = over
    sent[3 * KINDS : 4 * KINDS, :] = middle_sent[...]
    there = orders[HALF:PACKED, 2:3]
    bests = [
        half_earlier(best, rows, z2b, there)
        for rows, best in ((own, near_ref[0]), (m1, near_ref[1]), (m3, near_ref[2]), (m2, middle_ref[0]))
    ]
    for q, best, lines, places in (
        (0, bests[0], own_lines[0], own_hot[0]),
        (1, bests[1], ring_lines[0], ring_hot[0]),
        (2, bests[2], ring_lines[1], ring_hot[1]),
        (4, bests[3], middle_lines[0], middle_hot[0]),
    ):
        sent[q * KINDS : (q + 1) * KINDS, :] = to_owners(best, lines, places)
    out_ref[...] = jnp.broadcast_to(over[0:1, :], (512, 128))
    to_x = jnp.where(lax.axis_index("core") == 0, lax.axis_index("x"), lax.axis_index("y"))
    out_ref[pl.ds(pl.multiple_of(to_x * 128, 128), 128), :] = jnp.transpose(sent[...])


def final_kernel(in_ref, out_ref, over_ref, picked):
    my_x, my_core = lax.axis_index("x"), lax.axis_index("core")
    over = jnp.where(iota((512, 128), 1) == OVER, in_ref[...], 0.0)
    over_ref[0, 0] = (jnp.max(over) > 0.5).astype(I32)
    first = jnp.where(my_core == 0, my_x * 128, my_x * 8)
    step = jnp.where(my_core == 0, 8, 128)
    for z in range(4):
        for r in range(4):
            at = pl.multiple_of(first + z * 32 + r * step, 8)
            picked[(z * 4 + r) * 8 : (z * 4 + r) * 8 + 8, :] = in_ref[pl.ds(at, 8), :]
    got = jnp.transpose(picked[...])
    lane = iota((KINDS, 128), 1) % 32
    best = got[0:KINDS, :]
    for q, away in ((1, 3), (2, 1), (4, 2)):
        part = got[q * KINDS : (q + 1) * KINDS, :]
        moved = jnp.where(
            lane >= 8 * away,
            pltpu.roll(part, 8 * away, 1),
            pltpu.roll(part, 128 + 8 * away - 32, 1),
        )
        best = jnp.maximum(best, moved)
    part = got[3 * KINDS : 4 * KINDS, :]
    best = jnp.maximum(best, jnp.where(my_core == 0, pltpu.roll(part, 32, 1), pltpu.roll(part, 96, 1)))
    shift = lane // 8 - iota((KINDS, 128), 0) // 2
    turned = best
    for d in (-3, -2, -1, 1, 2, 3):
        moved = pltpu.roll(pltpu.roll(best, (8 - 2 * d) % 8, 0), (8 * d) % 128, 1)
        turned = jnp.where(shift == d, moved, turned)
    out_ref[...] = jnp.where(my_core == 0, best, turned)


def call(kernel, out, scratch=(), ins=None, outs=None, cost=None):
    more = {}
    if ins is not None:
        more["in_specs"] = ins
    if outs is not None:
        more["out_specs"] = outs
    return pl.pallas_call(
        kernel,
        out_shape=out,
        scratch_shapes=list(scratch),
        cost_estimate=cost,
        compiler_params=pltpu.CompilerParams(vmem_limit_bytes=VMEM),
        **more,
    )


def move(a, to):
    at = lambda x, c, z, y: ((x % 4 * 2 + c) * 4 + z % 4) * 4 + y % 4
    places = [(x, c, z, y) for x in range(4) for c in range(2) for z in range(4) for y in range(4)]
    return lax.ppermute(a, AXES, [(at(*p), at(*to(*p))) for p in places])


def across(a, step):
    return move(a, lambda x, c, z, y: (x + (1 - c) * step, c, z, y + c * step))


def along(a, step):
    return move(a, lambda x, c, z, y: (x + c * step, c, z, y + (1 - c) * step))


def down(a):
    return move(a, lambda x, c, z, y: (x, c, z - 1 + 2 * c, y))


def core_swap(a):
    return lax.ppermute(a, "core", [(0, 1), (1, 0)])


def fast(embeddings, cluster_id, row_order, assignment, placement):
    vmem = pl.BlockSpec(memory_space=pltpu.VMEM)
    smem = pl.BlockSpec(memory_space=pltpu.SMEM)
    line = lambda a: a.reshape(1, ROWS)
    cheap = pl.CostEstimate(flops=10**9, bytes_accessed=2 * 10**6, transcendentals=0)
    blocks = jax.ShapeDtypeStruct((4 * BLOCK, WIDTH), BF16)
    other, pool, target = call(
        prep_kernel,
        (
            blocks,
            jax.ShapeDtypeStruct((ROWS + 128, WIDTH), BF16),
            jax.ShapeDtypeStruct((8, ROWS + 128), F32),
        ),
        ins=[smem] + [vmem] * 4,
        cost=cheap,
    )(assignment, embeddings, line(cluster_id), line(row_order), line(placement))
    other = core_swap(other)
    same = call(same_kernel, blocks, cost=cheap)(pool, target)
    shape = (4, 1, BLOCK, WIDTH)
    both = jnp.concatenate([same.reshape(shape), other.reshape(shape)], axis=1).reshape(4, 2 * BLOCK, WIDTH)
    piece = jax.ShapeDtypeStruct((HALF, WIDTH), BF16)
    part = jax.ShapeDtypeStruct((PACKED, WIDTH), BF16)
    own, low, high, over = call(
        pack_kernel,
        (part, piece, piece, jax.ShapeDtypeStruct((8, 128), F32)),
        [pltpu.VMEM((KINDS * BLOCK, WIDTH), BF16)],
        cost=cheap,
    )(both[0], *[across(both[k], k) for k in (1, 2, 3)])
    z1a, z1b = down(low), down(high)
    m1, m3 = along(own, 1), along(own, -1)
    other_over = core_swap(over)
    z2a, z2b = down(z1a), down(z1b)
    m2a, m2b = along(m1[:HALF], 1), along(m3[HALF:], -1)
    product = 2 * PACKED * PACKED * WIDTH
    cost = lambda n: pl.CostEstimate(flops=n * product, bytes_accessed=6 * 10**6, transcendentals=0)
    order = pltpu.VMEM((PACKED, 8), F32)
    made = lambda n, k: (
        jax.ShapeDtypeStruct((n, 8, PACKED), F32),
        jax.ShapeDtypeStruct((k, 8, PACKED), F32),
        jax.ShapeDtypeStruct((k, PACKED, 128), BF16),
    )
    flag = jax.ShapeDtypeStruct((8, 128), F32)
    mine = call(own_kernel, made(1, 1), [order], cost=cost(1))(own)
    *ringed, over = call(ring_kernel, (*made(2, 2), flag), [order], cost=cost(2))(own, m1, m3, over, other_over)
    best, lines, hots = made(3, 1)
    z1, near, far_best, *z1_places = call(
        near_kernel, (part, best, jax.ShapeDtypeStruct((PACKED, 128), F32), lines, hots), [order], cost=cost(5)
    )(own, m1, m3, z1a, z1b, z2a, mine[0], ringed[0])
    best, lines, hots = made(1, 1)
    m2, *middle, orders = call(
        middle_kernel,
        (part, best, flag, lines, hots, jax.ShapeDtypeStruct((PACKED, 8), F32)),
        cost=cost(3),
    )(own, m2a, m2b, z1, z2a, far_best, *z1_places)
    back = call(
        far_kernel,
        jax.ShapeDtypeStruct((512, 128), F32),
        [pltpu.VMEM((128, 128), F32)],
        cost=cost(2),
    )(own, m1, m3, m2, z2b, *mine[1:], *ringed[1:], near, *middle, orders, over)
    back = lax.all_to_all(back, ("x", "z", "y"), split_axis=0, concat_axis=0, tiled=True)
    best, over = call(
        final_kernel,
        (jax.ShapeDtypeStruct((KINDS, 128), F32), jax.ShapeDtypeStruct((1, 1), I32)),
        [pltpu.VMEM((128, 128), F32)],
        ins=[vmem],
        outs=(vmem, smem),
    )(back)
    return best.reshape(KINDS * 128), over[0, 0] > 0


def slow(embeddings, cluster_id, row_order, assignment, placement):
    owners = KINDS * MEMBERS
    slots = owners * CAP
    wide = embeddings.astype(F32)
    mean = jnp.mean(wide * wide, axis=1, keepdims=True)
    unit = (wide * lax.rsqrt(mean + 1e-06) * (1.0 / math.sqrt(WIDTH))).astype(BF16)
    owner = jnp.sum(
        jnp.where(cluster_id[:, None] == jnp.arange(KINDS, dtype=I32)[None, :], assignment[None, :], 0), axis=1
    ) * MEMBERS + placement
    ids = jnp.arange(ROWS, dtype=I32)
    rank = jnp.sum(((owner[:, None] == owner[None, :]) & (ids[None, :] < ids[:, None])).astype(I32), axis=1)
    target = owner * CAP + rank
    units = jnp.zeros((slots, WIDTH), BF16).at[target].set(unit)
    orders = jnp.full((slots,), ROWS * owners, I32).at[target].set(row_order)
    swap = lambda a: lax.all_to_all(a, AXES, split_axis=0, concat_axis=0, tiled=True)
    units, orders = swap(units), swap(orders)

    def step(_, carried):
        best, piece, piece_orders = carried

        def block(packed):
            block_units, block_orders = packed
            scores = jnp.einsum("ik,jk->ij", block_units, piece, preferred_element_type=F32)
            fit = piece_orders[None, :] < block_orders[:, None]
            return jnp.max(jnp.where(fit, scores, -2.0), axis=1)

        here = lax.map(block, (units.reshape(2, slots // 2, WIDTH), orders.reshape(2, slots // 2)))
        best = jnp.maximum(best, here.reshape(slots))
        turn = [(i, (i + 1) % MEMBERS) for i in range(MEMBERS)]
        return best, lax.ppermute(piece, ("z", "y"), turn), lax.ppermute(piece_orders, ("z", "y"), turn)

    best = lax.fori_loop(0, MEMBERS, step, (jnp.full((slots,), -2.0, F32), units, orders))[0]
    return jnp.where(orders < ROWS * owners, jnp.maximum(best, -1.0), -1.0)


def local(*args):
    best, over = fast(*args)
    return lax.cond(over, lambda args, best: slow(*args), lambda args, best: best, args, best)


def solution(mesh):
    fine = Mesh(mesh.devices.reshape(4, 2, 4, 4), AXES)
    return jax.shard_map(
        local,
        mesh=fine,
        in_specs=(P(AXES, None), P(AXES), P(AXES), P(), P(AXES)),
        out_specs=P(AXES),
        check_vma=False,
    )
```

```python
import math

import jax
import jax.numpy as jnp
from jax import lax
from jax.experimental import pallas as pl
from jax.experimental.pallas import tpu as pltpu
from jax.sharding import Mesh
from jax.sharding import PartitionSpec as P

F32, BF16, I32 = jnp.float32, jnp.bfloat16, jnp.int32
AXES = ("x", "core", "z", "y")
WIDTH = 768
ROWS = 512
KINDS = 8
MEMBERS = 16
CAP = 8
SEND = 96
BLOCK = SEND + 8
PACKED = 640
HEAD = 16
HELD = PACKED - HEAD
HALF = PACKED // 2
FAR = 256.0
VMEM = 16 * 2**20


def iota(shape, axis):
    return lax.broadcasted_iota(I32, shape, axis)


def iota_f(shape, axis):
    return iota(shape, axis).astype(F32)


def hot(hits):
    return jnp.where(hits, 1.0, 0.0).astype(BF16)


def mul(a, b):
    return jnp.dot(a, b, preferred_element_type=F32)


def mul_nt(a, b):
    return lax.dot_general(a, b, (((1,), (1,)), ((), ())), preferred_element_type=F32)


def rows_of(*rows):
    n = next(r.shape[1] for r in rows if r is not None)
    at = iota((8, n), 0)
    out = jnp.zeros((8, n), F32)
    for i, row in enumerate(rows):
        if row is not None:
            out = jnp.where(at == i, jnp.broadcast_to(row, (8, n)), out)
    return out


def prep_kernel(assign_ref, emb_ref, cid_ref, order_ref, place_ref, other_ref, both_ref, target_ref):
    wide = emb_ref[...].astype(F32)
    mean = jnp.mean(wide * wide, axis=1, keepdims=True)
    unit = (wide * lax.rsqrt(mean + 1e-06) * (1.0 / math.sqrt(WIDTH))).astype(BF16)
    my_x, my_core, my_y = lax.axis_index("x"), lax.axis_index("core"), lax.axis_index("y")
    cid = cid_ref[...]
    group = jnp.zeros_like(cid)
    for c in range(KINDS):
        core = lax.rem(assign_ref[c], 2)
        away = lax.rem(assign_ref[c] // 2 - jnp.where(core == 0, my_x, my_y) + 4, 4)
        away += 4 * lax.rem(core + my_core, 2)
        group = jnp.where(cid == c, away, group)
    group = group.astype(F32)
    place = place_ref[...].astype(F32)
    owner = group * MEMBERS + place
    columns = jnp.transpose(rows_of(group, owner))
    before = iota((ROWS, ROWS), 0) < iota((ROWS, ROWS), 1)

    def rank(column, row):
        return jnp.sum(jnp.where(before & (column == row), 1.0, 0.0), axis=0, keepdims=True)

    in_group = rank(columns[:, 0:1], group)
    in_owner = rank(columns[:, 1:2], owner)
    fits = in_group < SEND
    order = order_ref[...]
    high = (order // 256).astype(F32)
    low = (order % 256).astype(F32)
    kind = jnp.where(iota_f((KINDS, ROWS), 0) == group, 1.0, 0.0)
    numbers = jnp.concatenate([kind * high, kind * low, kind * (place * CAP + in_owner + 1.0)], axis=0)
    slot = jnp.transpose(rows_of(in_group))[:, 0:1]
    spread = mul(numbers.astype(BF16), hot(iota_f((ROWS, 128), 1) == slot))
    spread = jnp.where(iota((24, 128), 1) < SEND, spread, 0.0)
    counts = jnp.zeros((KINDS, 128), F32)
    for c in range(KINDS):
        count = jnp.sum(jnp.where(cid == c, 1.0, 0.0), axis=1, keepdims=True)
        counts = jnp.where(iota((KINDS, 128), 1) == assign_ref[c], count, counts)
    numbers = jnp.concatenate([spread, counts, jnp.zeros((96, 128), F32)], axis=0)
    numbers = jnp.concatenate([numbers, jnp.zeros((128, WIDTH - 128), F32)], axis=1).astype(BF16)
    at = iota((1, 128), 1)
    at = jnp.where(at < 32, (at % 8) * BLOCK + SEND + at // 8, -1).astype(F32)
    target = jnp.concatenate([jnp.where(fits, group * BLOCK + in_group, -1.0), at], axis=1)
    both = jnp.concatenate([unit, numbers], axis=0)
    both_ref[...] = both
    target_ref[...] = jnp.broadcast_to(target, (8, ROWS + 128))
    half = 4 * BLOCK
    placing = hot(iota_f((half, ROWS + 128), 0) == target - half)
    other_ref[...] = mul(placing, both).astype(BF16)


def same_kernel(both_ref, target_ref, same_ref):
    placing = hot(iota_f((4 * BLOCK, ROWS + 128), 0) == target_ref[0:1, :])
    same_ref[...] = mul(placing, both_ref[...]).astype(BF16)


def pack_kernel(here_ref, from1_ref, from3_ref, from2_ref, out_ref, low_ref, high_ref, over_ref, in_ref):
    count = KINDS * BLOCK
    for k, ref in enumerate((here_ref, from1_ref, from2_ref, from3_ref)):
        in_ref[k * 2 * BLOCK : (k + 1) * 2 * BLOCK, :] = ref[...]
    my_core = lax.axis_index("core")
    my_line = jnp.where(my_core == 0, lax.axis_index("x"), lax.axis_index("y"))
    at = iota((32, count), 0)
    pick = hot(iota((32, count), 1) == (at % 8) * BLOCK + SEND + at // 8)
    numbers = mul(pick, in_ref[:, 0:128])
    n = jnp.sum(jnp.where(numbers[16:24, :] > 0.0, 1.0, 0.0), axis=1, keepdims=True)
    line = iota((KINDS, 1), 0)
    base = jnp.zeros((KINDS, 1), F32)
    source = jnp.zeros((KINDS, 1), F32)
    lane = iota_f((1, count), 1)
    position = jnp.full((1, count), -1.0, F32)
    start = jnp.full((1, 1), float(HEAD), F32)
    for b in range(KINDS):
        step = lane - b * BLOCK
        mine = n[b : b + 1, :]
        position = jnp.where((step >= 0.0) & (step < mine), start + step, position)
        base = jnp.where(line == b, start, base)
        from_device = 2 * lax.rem(my_line - b // 2 + 4, 4) + lax.rem(my_core + b % 2, 2)
        source = jnp.where(line == b, from_device.astype(F32), source)
        start = start + mine
    position = jnp.where(position < PACKED, position, -1.0)
    placing = hot(iota_f((HELD, count), 0) == position - HEAD)
    out_ref[HEAD:PACKED, :] = mul(placing, in_ref[...]).astype(BF16)
    step = iota_f((KINDS, PACKED), 1) - base
    mine = jnp.where((step >= 0.0) & (step < n), 1.0, 0.0)
    slot = jnp.sum(mine * step, axis=0, keepdims=True)
    found = mul(numbers[0:24, :].astype(BF16), hot(iota_f((128, PACKED), 0) == slot))
    high, low, code = (
        jnp.sum(mine * found[i * 8 : i * 8 + 8, :], axis=0, keepdims=True) for i in range(3)
    )
    source = jnp.sum(mine * source, axis=0, keepdims=True)
    counts = numbers[24:32, :]
    over = jnp.max(jnp.where(counts > SEND, 1.0, 0.0), axis=0, keepdims=True)
    ours = iota((1, 128), 1) % 2 == my_core
    full = ours & (jnp.sum(counts, axis=0, keepdims=True) > HELD)
    over = jnp.maximum(over, jnp.where(full, 1.0, 0.0))
    over = jnp.max(over, axis=1, keepdims=True)
    valid = code > 0.0
    final = rows_of(
        jnp.where(valid, high, FAR),
        jnp.where(valid, low, 0.0),
        jnp.where(valid, code, 0.0),
        jnp.where(valid, source, 0.0),
    )
    over_ref[...] = jnp.broadcast_to(over, (8, 128))
    final = jnp.concatenate([final, jnp.zeros((8, WIDTH - PACKED), F32)], axis=1)
    final = jnp.concatenate([final, jnp.zeros((8, WIDTH), F32)], axis=0)
    out_ref[0:HEAD, :] = final.astype(BF16)
    low_ref[...] = out_ref[0:HALF, :]
    high_ref[...] = out_ref[HALF:PACKED, :]


def numbers_of(ref):
    return ref[0:HEAD, :].astype(F32)[0:8, 0:PACKED]


def orders_of(numbers):
    return numbers[0:1, :] * 256.0 + numbers[1:2, :]


def earlier_max(best, rows_ref, row_order, cols_ref, col_order):
    scores = mul_nt(cols_ref[...], rows_ref[...])
    scores = jnp.where(col_order < row_order, scores, -2.0)
    count, n = scores.shape
    return jnp.maximum(best, jnp.max(scores.reshape(count // 8, 8, n), axis=0))


def orders_down(*refs):
    return jnp.transpose(rows_of(*[orders_of(numbers_of(r)) for r in refs]))


def all_earlier(best, rows, cols, orders, first):
    order = orders_of(numbers_of(rows))
    for k, col in enumerate(cols):
        best = earlier_max(best, rows, order, col, orders[:, first + k : first + k + 1])
    return best


def nothing():
    return jnp.full((8, PACKED), -2.0, F32)


def owner_lines(numbers, lines_ref, hot_ref, q):
    lines_ref[q] = jnp.where((iota_f((KINDS, PACKED), 0) == numbers[3:4, :]) & (numbers[2:3, :] > 0.0), 1.0, 0.0)
    code = jnp.transpose(rows_of(numbers[2:3, :]))[:, 0:1]
    hot_ref[q] = hot(iota_f((PACKED, 128), 1) == code - 1.0)


def half_earlier(best, rows, half, order):
    return earlier_max(best, rows, orders_of(numbers_of(rows)), half, order)


def both_ways(best, far_best, rows, z1, z1_order):
    scores = mul_nt(z1[...], rows[...])
    earlier = z1_order < orders_of(numbers_of(rows))
    count, n = scores.shape
    ours = jnp.where(earlier, scores, -2.0)
    theirs = jnp.where(earlier, -2.0, scores)
    for k in range(n // 128):
        far_best = jnp.maximum(far_best, theirs[:, k * 128 : (k + 1) * 128])
    return jnp.maximum(best, jnp.max(ours.reshape(count // 8, 8, n), axis=0)), far_best


def own_kernel(own, best_ref, lines_ref, hot_ref, order_ref):
    order_ref[...] = orders_down(own)
    best_ref[0] = all_earlier(nothing(), own, (own,), order_ref, 0)
    owner_lines(numbers_of(own), lines_ref, hot_ref, 0)


def pass_kernel(part, own_best, out_ref):
    out_ref[...] = part[...]


def ring_kernel(own, m1, m3, over_a, over_b, best_ref, lines_ref, hot_ref, over_ref, order_ref):
    order_ref[...] = orders_down(own)
    for i, rows in enumerate((m1, m3)):
        best_ref[i] = all_earlier(nothing(), rows, (own,), order_ref, 0)
        owner_lines(numbers_of(rows), lines_ref, hot_ref, i)
    over_ref[...] = jnp.maximum(over_a[...], over_b[...])


def near_kernel(own, m1, m3, z1a, z1b, z2a, own_ref, ring_ref, z1, best_ref, far_best_ref, lines_ref, hot_ref, order_ref):
    z1[0:HALF, :] = z1a[...]
    z1[HALF:PACKED, :] = z1b[...]
    order_ref[...] = orders_down(z1, z2a)
    far_best = jnp.full((PACKED, 128), -2.0, F32)
    for i, (rows, best) in enumerate(((own, own_ref[0]), (m1, ring_ref[0]), (m3, ring_ref[1]))):
        best, far_best = both_ways(best, far_best, rows, z1, order_ref[:, 0:1])
        best_ref[i] = half_earlier(best, rows, z2a, order_ref[0:HALF, 1:2])
    far_best_ref[...] = far_best
    owner_lines(numbers_of(z1), lines_ref, hot_ref, 0)


def middle_kernel(
    own, m2a, m2b, z1, z2a, far_best_ref, z1_lines, z1_hot, m2, best_ref, sent_ref, lines_ref, hot_ref, order_ref
):
    m2[0:HALF, :] = m2a[...]
    m2[HALF:PACKED, :] = m2b[...]
    order_ref[...] = orders_down(z1, own, z2a)
    best, far_best = both_ways(nothing(), far_best_ref[...], m2, z1, order_ref[:, 0:1])
    far_best = jnp.max(far_best, axis=1, keepdims=True)
    far_best = jnp.transpose(jnp.broadcast_to(far_best, (PACKED, 8)))
    best = all_earlier(best, m2, (own,), order_ref, 1)
    best_ref[0] = half_earlier(best, m2, z2a, order_ref[0:HALF, 2:3])
    sent_ref[...] = to_owners(far_best, z1_lines[0], z1_hot[0])
    owner_lines(numbers_of(m2), lines_ref, hot_ref, 0)


def to_owners(best, lines, places):
    best = jnp.maximum(jnp.max(best, axis=0, keepdims=True), -1.0)
    high = best.astype(BF16).astype(F32)
    low = best - high
    middle = low.astype(BF16).astype(F32)
    low = low - middle
    pieces = jnp.concatenate([lines, lines * high, lines * middle, lines * low], axis=0)
    put = mul(pieces.astype(BF16), places)
    return (put[0:8, :] - 1.0) + (put[8:16, :] + put[16:24, :] + put[24:32, :])


OVER = 5 * KINDS


def far_kernel(
    own, m1, m3, m2, z2b, own_lines, own_hot, ring_lines, ring_hot, near_ref,
    middle_ref, middle_sent, middle_lines, middle_hot, orders, over_ref, out_ref, sent,
):
    sent[...] = jnp.zeros((128, 128), F32)
    over = over_ref[...]
    sent[OVER : OVER + 8, :] = over
    sent[3 * KINDS : 4 * KINDS, :] = middle_sent[...]
    there = orders[HALF:PACKED, 2:3]
    bests = [
        half_earlier(best, rows, z2b, there)
        for rows, best in ((own, near_ref[0]), (m1, near_ref[1]), (m3, near_ref[2]), (m2, middle_ref[0]))
    ]
    for q, best, lines, places in (
        (0, bests[0], own_lines[0], own_hot[0]),
        (1, bests[1], ring_lines[0], ring_hot[0]),
        (2, bests[2], ring_lines[1], ring_hot[1]),
        (4, bests[3], middle_lines[0], middle_hot[0]),
    ):
        sent[q * KINDS : (q + 1) * KINDS, :] = to_owners(best, lines, places)
    out_ref[...] = jnp.broadcast_to(over[0:1, :], (512, 128))
    to_x = jnp.where(lax.axis_index("core") == 0, lax.axis_index("x"), lax.axis_index("y"))
    out_ref[pl.ds(pl.multiple_of(to_x * 128, 128), 128), :] = jnp.transpose(sent[...])


def final_kernel(in_ref, out_ref, over_ref, picked):
    my_x, my_core = lax.axis_index("x"), lax.axis_index("core")
    over = jnp.where(iota((512, 128), 1) == OVER, in_ref[...], 0.0)
    over_ref[0, 0] = (jnp.max(over) > 0.5).astype(I32)
    first = jnp.where(my_core == 0, my_x * 128, my_x * 8)
    step = jnp.where(my_core == 0, 8, 128)
    for z in range(4):
        for r in range(4):
            at = pl.multiple_of(first + z * 32 + r * step, 8)
            picked[(z * 4 + r) * 8 : (z * 4 + r) * 8 + 8, :] = in_ref[pl.ds(at, 8), :]
    got = jnp.transpose(picked[...])
    lane = iota((KINDS, 128), 1) % 32
    best = got[0:KINDS, :]
    for q, away in ((1, 3), (2, 1), (4, 2)):
        part = got[q * KINDS : (q + 1) * KINDS, :]
        moved = jnp.where(
            lane >= 8 * away,
            pltpu.roll(part, 8 * away, 1),
            pltpu.roll(part, 128 + 8 * away - 32, 1),
        )
        best = jnp.maximum(best, moved)
    part = got[3 * KINDS : 4 * KINDS, :]
    best = jnp.maximum(best, jnp.where(my_core == 0, pltpu.roll(part, 32, 1), pltpu.roll(part, 96, 1)))
    shift = lane // 8 - iota((KINDS, 128), 0) // 2
    turned = best
    for d in (-3, -2, -1, 1, 2, 3):
        moved = pltpu.roll(pltpu.roll(best, (8 - 2 * d) % 8, 0), (8 * d) % 128, 1)
        turned = jnp.where(shift == d, moved, turned)
    out_ref[...] = jnp.where(my_core == 0, best, turned)


def call(kernel, out, scratch=(), ins=None, outs=None, cost=None):
    more = {}
    if ins is not None:
        more["in_specs"] = ins
    if outs is not None:
        more["out_specs"] = outs
    return pl.pallas_call(
        kernel,
        out_shape=out,
        scratch_shapes=list(scratch),
        cost_estimate=cost,
        compiler_params=pltpu.CompilerParams(vmem_limit_bytes=VMEM),
        **more,
    )


def move(a, to):
    at = lambda x, c, z, y: ((x % 4 * 2 + c) * 4 + z % 4) * 4 + y % 4
    places = [(x, c, z, y) for x in range(4) for c in range(2) for z in range(4) for y in range(4)]
    return lax.ppermute(a, AXES, [(at(*p), at(*to(*p))) for p in places])


def across(a, step):
    return move(a, lambda x, c, z, y: (x + (1 - c) * step, c, z, y + c * step))


def along(a, step):
    return move(a, lambda x, c, z, y: (x + c * step, c, z, y + (1 - c) * step))


def down(a):
    return move(a, lambda x, c, z, y: (x, c, z - 1 + 2 * c, y))


def core_swap(a):
    return lax.ppermute(a, "core", [(0, 1), (1, 0)])


def fast(embeddings, cluster_id, row_order, assignment, placement):
    vmem = pl.BlockSpec(memory_space=pltpu.VMEM)
    smem = pl.BlockSpec(memory_space=pltpu.SMEM)
    line = lambda a: a.reshape(1, ROWS)
    cheap = pl.CostEstimate(flops=10**9, bytes_accessed=2 * 10**6, transcendentals=0)
    blocks = jax.ShapeDtypeStruct((4 * BLOCK, WIDTH), BF16)
    other, pool, target = call(
        prep_kernel,
        (
            blocks,
            jax.ShapeDtypeStruct((ROWS + 128, WIDTH), BF16),
            jax.ShapeDtypeStruct((8, ROWS + 128), F32),
        ),
        ins=[smem] + [vmem] * 4,
        cost=cheap,
    )(assignment, embeddings, line(cluster_id), line(row_order), line(placement))
    other = core_swap(other)
    same = call(same_kernel, blocks, cost=cheap)(pool, target)
    shape = (4, 1, BLOCK, WIDTH)
    both = jnp.concatenate([same.reshape(shape), other.reshape(shape)], axis=1).reshape(4, 2 * BLOCK, WIDTH)
    arrived = [across(both[k], k) for k in (2, 1, 3)]
    piece = jax.ShapeDtypeStruct((HALF, WIDTH), BF16)
    part = jax.ShapeDtypeStruct((PACKED, WIDTH), BF16)
    own, low, high, over = call(
        pack_kernel,
        (part, piece, piece, jax.ShapeDtypeStruct((8, 128), F32)),
        [pltpu.VMEM((KINDS * BLOCK, WIDTH), BF16)],
        cost=cheap,
    )(both[0], *arrived[1:], arrived[0])
    z1a, z1b = down(low), down(high)
    m1, m3 = along(own, 1), along(own, -1)
    other_over = core_swap(over)
    z2b = down(z1b)
    m2a, m2b = along(m1[:HALF], 1), along(m3[HALF:], -1)
    product = 2 * PACKED * PACKED * WIDTH
    cost = lambda n: pl.CostEstimate(flops=n * product, bytes_accessed=6 * 10**6, transcendentals=0)
    order = pltpu.VMEM((PACKED, 8), F32)
    made = lambda n, k: (
        jax.ShapeDtypeStruct((n, 8, PACKED), F32),
        jax.ShapeDtypeStruct((k, 8, PACKED), F32),
        jax.ShapeDtypeStruct((k, PACKED, 128), BF16),
    )
    flag = jax.ShapeDtypeStruct((8, 128), F32)
    mine = call(own_kernel, made(1, 1), [order], cost=cost(1))(own)
    z2a = down(call(pass_kernel, piece)(z1a, mine[0]))
    *ringed, over = call(ring_kernel, (*made(2, 2), flag), [order], cost=cost(2))(own, m1, m3, over, other_over)
    best, lines, hots = made(3, 1)
    z1, near, far_best, *z1_places = call(
        near_kernel, (part, best, jax.ShapeDtypeStruct((PACKED, 128), F32), lines, hots), [order], cost=cost(5)
    )(own, m1, m3, z1a, z1b, z2a, mine[0], ringed[0])
    best, lines, hots = made(1, 1)
    m2, *middle, orders = call(
        middle_kernel,
        (part, best, flag, lines, hots, jax.ShapeDtypeStruct((PACKED, 8), F32)),
        cost=cost(3),
    )(own, m2a, m2b, z1, z2a, far_best, *z1_places)
    back = call(
        far_kernel,
        jax.ShapeDtypeStruct((512, 128), F32),
        [pltpu.VMEM((128, 128), F32)],
        cost=cost(2),
    )(own, m1, m3, m2, z2b, *mine[1:], *ringed[1:], near, *middle, orders, over)
    back = lax.all_to_all(back, ("x", "z", "y"), split_axis=0, concat_axis=0, tiled=True)
    best, over = call(
        final_kernel,
        (jax.ShapeDtypeStruct((KINDS, 128), F32), jax.ShapeDtypeStruct((1, 1), I32)),
        [pltpu.VMEM((128, 128), F32)],
        ins=[vmem],
        outs=(vmem, smem),
    )(back)
    return best.reshape(KINDS * 128), over[0, 0] > 0


def slow(embeddings, cluster_id, row_order, assignment, placement):
    owners = KINDS * MEMBERS
    slots = owners * CAP
    wide = embeddings.astype(F32)
    mean = jnp.mean(wide * wide, axis=1, keepdims=True)
    unit = (wide * lax.rsqrt(mean + 1e-06) * (1.0 / math.sqrt(WIDTH))).astype(BF16)
    owner = jnp.sum(
        jnp.where(cluster_id[:, None] == jnp.arange(KINDS, dtype=I32)[None, :], assignment[None, :], 0), axis=1
    ) * MEMBERS + placement
    ids = jnp.arange(ROWS, dtype=I32)
    rank = jnp.sum(((owner[:, None] == owner[None, :]) & (ids[None, :] < ids[:, None])).astype(I32), axis=1)
    target = owner * CAP + rank
    units = jnp.zeros((slots, WIDTH), BF16).at[target].set(unit)
    orders = jnp.full((slots,), ROWS * owners, I32).at[target].set(row_order)
    swap = lambda a: lax.all_to_all(a, AXES, split_axis=0, concat_axis=0, tiled=True)
    units, orders = swap(units), swap(orders)

    def step(_, carried):
        best, piece, piece_orders = carried

        def block(packed):
            block_units, block_orders = packed
            scores = jnp.einsum("ik,jk->ij", block_units, piece, preferred_element_type=F32)
            fit = piece_orders[None, :] < block_orders[:, None]
            return jnp.max(jnp.where(fit, scores, -2.0), axis=1)

        here = lax.map(block, (units.reshape(2, slots // 2, WIDTH), orders.reshape(2, slots // 2)))
        best = jnp.maximum(best, here.reshape(slots))
        turn = [(i, (i + 1) % MEMBERS) for i in range(MEMBERS)]
        return best, lax.ppermute(piece, ("z", "y"), turn), lax.ppermute(piece_orders, ("z", "y"), turn)

    best = lax.fori_loop(0, MEMBERS, step, (jnp.full((slots,), -2.0, F32), units, orders))[0]
    return jnp.where(orders < ROWS * owners, jnp.maximum(best, -1.0), -1.0)


def local(*args):
    best, over = fast(*args)
    return lax.cond(over, lambda args, best: slow(*args), lambda args, best: best, args, best)


def solution(mesh):
    fine = Mesh(mesh.devices.reshape(4, 2, 4, 4), AXES)
    return jax.shard_map(
        local,
        mesh=fine,
        in_specs=(P(AXES, None), P(AXES), P(AXES), P(), P(AXES)),
        out_specs=P(AXES),
        check_vma=False,
    )
```
